256 devices in a mesh: dp: 8 (over y, core), ctx: 32 (over z, x).
Axes of the slice: x: 4, y: 4, z: 8, core: 2. Of those that a mesh axis runs over, the one named last changes fastest.
Arguments:
- kv_latent: bfloat16 [8, 4096, 576], P('dp', 'ctx'), may hold values from -6.1 to 6.1
- q_nope: bfloat16 [8, 4096, 512], P('dp', 'ctx'), may hold values from -6 to 6
- q_rope: bfloat16 [8, 4096, 256], P('dp', 'ctx'), may hold values from -430 to 430
- w_key_up: bfloat16 [512, 512], replicated, may hold values from -0.25 to 0.25
- w_value_up: bfloat16 [512, 512], replicated, may hold values from -0.25 to 0.25
- out_grad: bfloat16 [8, 4096, 512], P('dp', 'ctx'), may hold values from -6 to 6
- segment_ids: int32 [8, 4096], P('dp', 'ctx'), may hold values from 0 to 9, never falling along the last dimension, each value on 1 to 1536 neighbouring positions
Outputs:
- grad_q_nope: bfloat16 [8, 4096, 512], P('dp', 'ctx')
- grad_q_rope: bfloat16 [8, 4096, 256], P('dp', 'ctx')
- grad_latent: bfloat16 [8, 4096, 576], P('dp', 'ctx')
- grad_w_key_up: float32 [512, 512], P('ctx')
- grad_w_value_up: float32 [512, 512], P('ctx')
The draws below stay inside these ranges and needn't reach their ends.
Inputs may be any that keep to these rules, and one draw needn't show every extreme that they name: `segment_ids`: ids never fall along a sequence; each document holds at most 1536 positions and some document holds exactly 1536.
All inputs are finite; a program needn't handle non-finite values.
Results may differ from the reference program's by a relative error of at most 0.039.
Values may be sent and summed in bfloat16 or wider, within the bound.
No kernel may reach another device: no remote copies, remote signals or barrier semaphores. Data moves between devices by JAX's collectives and lax.ppermute only.
A program may use at most 128 MiB of HBM per device.

```python
import math
import jax
import jax.numpy as jnp
import numpy as np
from jax import lax

LATENT = 512
ROPE = 64
HEAD = 128
HEADS = 4
BATCH = 8
SEQ = 4096
DOC_MOST = 1536
DOCS = 10


def shared_rope(key, nearness):
    base_rope = jnp.clip(jax.random.normal(key, (BATCH, SEQ, ROPE), jnp.float32), -6.0, 6.0)
    chosen = jax.random.uniform(jax.random.fold_in(key, 11), (BATCH, SEQ)) < 1.0 / 64.0
    ahead_mask = jnp.roll(chosen, -1, axis=1) & (nearness > 0.5)
    following = jnp.roll(base_rope, -1, axis=1)
    rope_rows = jnp.where(ahead_mask[..., None], following * 1.009, base_rope)
    return rope_rows


def draw_kv_latent(key, part):
    nearness = 0.0
    rope_rows = shared_rope(key, nearness)
    key = jax.random.fold_in(key, 3)
    latents = jnp.clip(jax.random.normal(key, (BATCH, SEQ, LATENT), jnp.float32), -6.0, 6.0)
    return jnp.concatenate([latents, rope_rows], axis=-1).astype(jnp.bfloat16)


def draw_q_rope(key, part):
    key = jax.random.fold_in(key, 5)
    queries = jnp.clip(jax.random.normal(key, (BATCH, SEQ, HEADS, ROPE), jnp.float32), -6.0, 6.0)
    return queries.reshape(BATCH, SEQ, HEADS * ROPE).astype(jnp.bfloat16)


def with_spikes(entries, own_key, source, target, blocks, factor):
    def block_of(dim):
        return (jnp.arange(entries.shape[dim]) // (entries.shape[dim] // blocks)).reshape((-1,) + (1,) * (entries.ndim - 1 - dim))

    first = jax.random.permutation(own_key, blocks)[block_of(target)]
    far = (block_of(target) + blocks // 2) % blocks
    return jnp.where((block_of(source) == first) | (block_of(source) == far), factor * entries, entries)


def shard_levels(own_key, extent, pieces, low, largest):
    loudness = 1.0
    for position, parts in pieces:
        steps = jax.random.uniform(jax.random.fold_in(jax.random.fold_in(own_key, 6), position), (parts,), jnp.float32, low / len(pieces), largest / len(pieces))
        loudness = loudness * jnp.repeat(jnp.exp(steps), extent[position] // parts).reshape((-1,) + (1,) * (len(extent) - 1 - position))
    return loudness


def length_profile(number_of, total, limit, lean):
    portions = [(1 << 20) // math.isqrt(standing ** lean) + 1 for standing in range(2, number_of + 1)]
    spare, given = total - limit - (number_of - 1), [1] * (number_of - 1)
    while spare > 0:
        movable = [i for i in range(number_of - 1) if given[i] < limit]
        pool, budget = sum([portions[i] for i in movable]), spare
        for i in movable:
            extra = min(limit - given[i], max(1, budget * portions[i] // pool), spare)
            given[i] = given[i] + extra
            spare = spare - extra
    return np.array([limit] + given)


def ragged_sizes(rng, count, total, bound, skew):
    if count == 2:
        one = jax.random.randint(rng, (), max(1, total - bound), min(bound, total - 1) + 1)
        return jnp.stack([one, total - one])
    lengths = jnp.asarray(length_profile(count, total, bound, skew), jnp.int32)
    couples = (count - 1) // 2
    donor, sink = lengths[1:1 + 2 * couples:2], lengths[2:2 + 2 * couples:2]
    slack = jnp.minimum(donor - 1, bound - sink)
    shifted = jax.random.randint(jax.random.fold_in(rng, 1), (couples,), 0, 1 << 20) % (slack + 1)
    lengths = lengths.at[1:1 + 2 * couples:2].set(donor - shifted).at[2:2 + 2 * couples:2].set(sink + shifted)
    return lengths[jax.random.permutation(jax.random.fold_in(rng, 2), count)]


def normal_values(stream_key, shape, deviation, reach, pieces=(), held_as=jnp.bfloat16):
    entries = deviation * jax.random.normal(stream_key, shape, jnp.float32)
    if pieces:
        entries = entries * shard_levels(stream_key, shape, pieces, -0.22, 0.18)
    return jnp.clip(entries, -reach, reach).astype(held_as)


def gaussian_with(own_key, dims, width, reach, split, heavy, kind=jnp.bfloat16):
    entries = width * jax.random.normal(own_key, dims, jnp.float32)
    if split:
        entries = entries * shard_levels(own_key, dims, split, -0.22, 0.18)
    return jnp.clip(with_spikes(entries, jax.random.fold_in(own_key, 3), *heavy), -reach, reach).astype(kind)


def setup_inputs(seed: int = 0) -> dict:
    streams_of = jax.random.split(jax.random.key(seed), 8)
    kv_latent = draw_kv_latent(jax.random.fold_in(streams_of[7], 71), 0)
    q_nope = gaussian_with(streams_of[1], (BATCH, SEQ, HEADS * HEAD), 1.0, 6.0, ((0, 8), (1, 32)), (1, 2, 32, 2.75))
    q_rope = draw_q_rope(jax.random.fold_in(streams_of[7], 71), 0)
    w_key_up = normal_values(streams_of[3], (LATENT, HEADS * HEAD), LATENT ** -0.5, 0.25)
    w_value_up = normal_values(streams_of[4], (LATENT, HEADS * HEAD), LATENT ** -0.5, 0.25)
    out_grad = gaussian_with(streams_of[5], (BATCH, SEQ, HEADS * HEAD), 1.0, 6.0, ((0, 8), (1, 32)), (1, 2, 32, 2.75))
    segment_ids = jax.vmap(lambda own: jnp.searchsorted(jnp.cumsum(ragged_sizes(own, DOCS, SEQ, DOC_MOST, 2)), jnp.arange(SEQ), side="right"))(jax.random.split(streams_of[6], BATCH)).reshape((BATCH, SEQ)).astype(jnp.int32)
    return {"kv_latent": kv_latent, "q_nope": q_nope, "q_rope": q_rope, "w_key_up": w_key_up, "w_value_up": w_value_up, "out_grad": out_grad, "segment_ids": segment_ids}


def product(pattern, left_operand, right_operand):
    return jnp.einsum(pattern, left_operand.astype(jnp.float32), right_operand.astype(jnp.float32), precision=lax.Precision.HIGHEST)


def block_grads(window, window_marks, key_pos, query_nope, query_rope, out_grads, query_marks, query_pos, key_up, value_up):
    latent_width = key_up.shape[0]
    latents = window[:, :latent_width]
    rope_keys = window[:, latent_width:]
    score_scale = (query_nope.shape[2] + query_rope.shape[2]) ** -0.5
    key_rows = product('kl,lhd->khd', latents, key_up).astype(jnp.bfloat16)
    query_latent = product('thd,lhd->thl', query_nope, key_up).astype(jnp.bfloat16)
    out_latent = product('thd,lhd->thl', out_grads, value_up).astype(jnp.bfloat16)
    scores = (product('thd,khd->htk', query_nope, key_rows) + product('thr,kr->htk', query_rope, rope_keys)) * score_scale
    allowed = (key_pos[None, :] <= query_pos[:, None]) & (window_marks[None, :] == query_marks[:, None])
    scores = jnp.where(allowed[None], scores, -jnp.inf)
    row_max = jnp.max(scores, axis=-1, keepdims=True)
    weights = jnp.exp(scores - row_max)
    attention = weights / jnp.sum(weights, axis=-1, keepdims=True)
    attention_low = attention.astype(jnp.bfloat16)
    dprob = product('thl,kl->htk', out_latent, latents)
    row_delta = jnp.sum(attention * dprob, axis=-1, keepdims=True)
    score_grad = (attention * (dprob - row_delta) * score_scale).astype(jnp.bfloat16)
    grad_nope = product('htk,khd->thd', score_grad, key_rows)
    grad_rope = product('htk,kr->thr', score_grad, rope_keys)
    latent_part = product('htk,thl->kl', score_grad, query_latent) + product('htk,thl->kl', attention_low, out_latent)
    rope_part = product('htk,thr->kr', score_grad, query_rope)
    latent_mix = product('htk,kl->thl', score_grad, latents).astype(jnp.bfloat16)
    value_mix = product('htk,kl->thl', attention_low, latents).astype(jnp.bfloat16)
    grad_key_up = product('thd,thl->hdl', query_nope, latent_mix)
    grad_value_up = product('thd,thl->hdl', out_grads, value_mix)
    return grad_nope, grad_rope, jnp.concatenate([latent_part, rope_part], axis=1), grad_key_up, grad_value_up


def one_row(latent_rows, nope_rows, rope_rows, grad_rows, segment_row, key_up, value_up):
    seq_len = latent_rows.shape[0]
    block_rows = min(512, seq_len)
    front_rows = DOC_MOST
    padded = jnp.concatenate([jnp.zeros((front_rows, LATENT + ROPE), latent_rows.dtype), latent_rows], axis=0)
    padded_marks = jnp.concatenate([jnp.zeros((front_rows,), jnp.int32), segment_row + 1])
    nope_three = nope_rows.reshape(seq_len, HEADS, HEAD)
    rope_three = rope_rows.reshape(seq_len, HEADS, ROPE)
    grad_three = grad_rows.reshape(seq_len, HEADS, HEAD)

    def step(state_now, first_row):
        latent_total, key_total, value_total = state_now
        window = lax.dynamic_slice_in_dim(padded, first_row, front_rows + block_rows, 0)
        window_marks = lax.dynamic_slice_in_dim(padded_marks, first_row, front_rows + block_rows, 0)
        key_pos = first_row - front_rows + jnp.arange(front_rows + block_rows, dtype=jnp.int32)
        query_pos = first_row + jnp.arange(block_rows, dtype=jnp.int32)
        query_nope = lax.dynamic_slice_in_dim(nope_three, first_row, block_rows, 0)
        query_rope = lax.dynamic_slice_in_dim(rope_three, first_row, block_rows, 0)
        out_grads = lax.dynamic_slice_in_dim(grad_three, first_row, block_rows, 0)
        query_marks = lax.dynamic_slice_in_dim(segment_row + 1, first_row, block_rows, 0)
        grad_nope, grad_rope, window_grad, block_key, block_value = block_grads(
            window, window_marks, key_pos, query_nope, query_rope, out_grads, query_marks, query_pos, key_up, value_up)
        previous = lax.dynamic_slice_in_dim(latent_total, first_row, front_rows + block_rows, 0)
        latent_total = lax.dynamic_update_slice_in_dim(latent_total, previous + window_grad, first_row, 0)
        return (latent_total, key_total + block_key, value_total + block_value), (grad_nope.astype(jnp.bfloat16), grad_rope.astype(jnp.bfloat16))

    initial = (jnp.zeros((front_rows + seq_len, LATENT + ROPE), jnp.float32),
               jnp.zeros((HEADS, HEAD, LATENT), jnp.float32),
               jnp.zeros((HEADS, HEAD, LATENT), jnp.float32))
    first_rows = jnp.arange(seq_len // block_rows, dtype=jnp.int32) * block_rows
    (latent_total, key_total, value_total), (grad_nope, grad_rope) = lax.scan(step, initial, first_rows)
    return (grad_nope.reshape(seq_len, HEADS * HEAD), grad_rope.reshape(seq_len, HEADS * ROPE),
            latent_total[front_rows:].astype(jnp.bfloat16), key_total, value_total)


def reference(kv_latent, q_nope, q_rope, w_key_up, w_value_up, out_grad, segment_ids):
    key_up = w_key_up.reshape(LATENT, HEADS, HEAD)
    value_up = w_value_up.reshape(LATENT, HEADS, HEAD)

    def run_row(row_args):
        return one_row(row_args[0], row_args[1], row_args[2], row_args[3], row_args[4], key_up, value_up)

    grad_nope, grad_rope, grad_lat, key_parts, value_parts = lax.map(run_row, (kv_latent, q_nope, q_rope, out_grad, segment_ids))
    grad_key = jnp.sum(key_parts, axis=0).reshape(HEADS * HEAD, LATENT)
    grad_value = jnp.sum(value_parts, axis=0).reshape(HEADS * HEAD, LATENT)
    return grad_nope, grad_rope, grad_lat, grad_key, grad_value
```

```python
import functools

import jax
import jax.numpy as jnp
from jax import lax
from jax.experimental import pallas as pl
from jax.experimental.pallas import tpu as pltpu
from jax.sharding import PartitionSpec as P

Z, X, Y = 8, 4, 4
HEADS, HEAD, ROPE, LATENT = 4, 128, 64, 512
ROWS = 128
REACH = 4
QROWS = X * ROWS
KROWS = REACH * ROWS
SCALE = (HEAD + ROPE) ** -0.5
NEG = -1e30
BF, F32 = jnp.bfloat16, jnp.float32
NT = (((1,), (1,)), ((), ()))
TN = (((0,), (0,)), ((), ()))
VMEM = pl.BlockSpec(memory_space=pltpu.VMEM)
SMEM = pl.BlockSpec(memory_space=pltpu.SMEM)


def x_shift(v, s):
    return lax.ppermute(v, "ctx", [(i, i // X * X + (i % X + s) % X) for i in range(Z * X)])


def z_shift(v, s):
    return lax.ppermute(v, "ctx", [(i, (i + s * X) % (Z * X)) for i in range(Z * X)])


def y_shift(v, s):
    return lax.ppermute(v, "dp", [(i, (i + 2 * s) % (2 * Y)) for i in range(2 * Y)])


def core_swap(v):
    return lax.ppermute(v, "dp", [(i, i ^ 1) for i in range(2 * Y)])


def call(kernel, out_shape, n_smem, n_vmem, scratch=(), flops=0, nbytes=0):
    return pl.pallas_call(
        kernel,
        out_shape=out_shape,
        in_specs=[SMEM] * n_smem + [VMEM] * n_vmem,
        out_specs=jax.tree.map(lambda _: VMEM, out_shape),
        scratch_shapes=list(scratch),
        compiler_params=pltpu.CompilerParams(vmem_limit_bytes=48 * 1024 * 1024),
        cost_estimate=pl.CostEstimate(flops=flops, bytes_accessed=nbytes, transcendentals=0),
    )


def pack_kernel(nope, rope, grad, kv, ids, q_out, c_out):
    for h in range(HEADS):
        q_out[h * 128:(h + 1) * 128, :] = nope[:, h * 128:(h + 1) * 128]
        q_out[512 + h * 128:512 + (h + 1) * 128, :] = grad[:, h * 128:(h + 1) * 128]
    for p in range(2):
        q_out[1024 + p * 128:1024 + (p + 1) * 128, :] = rope[:, p * 128:(p + 1) * 128]
    marks = jnp.broadcast_to(ids[...].astype(F32), (128, 128))
    q_out[1280:1296, :] = marks[:16].astype(BF)
    c_out[:, :512] = kv[:, :512]
    c_out[:, 512:640] = jnp.concatenate([kv[:, 512:576], marks.T[:, :64].astype(BF)], axis=1)


def pack(nope, rope, grad, kv, ids):
    return call(
        pack_kernel,
        (jax.ShapeDtypeStruct((1296, 128), BF), jax.ShapeDtypeStruct((128, 640), BF)),
        0, 5, nbytes=1 << 20,
    )(nope, rope, grad, kv, ids)


def stats_kernel(where, q0, q1, q2, q3, c0, c1, c2, c3, wk, wv, qc, gs, kc, vs, bias, stats, qid):
    xi, zi = where[0], where[1]
    for s, ref in enumerate((q0, q1, q2, q3)):
        at = pl.ds(pl.multiple_of(((xi + s) & 3) * 128, 128), 128)
        for h in range(HEADS):
            qc[h, at, 0:128] = ref[h * 128:(h + 1) * 128, :]
            qc[h, at, 128:256] = ref[1024 + h // 2 * 128:1152 + h // 2 * 128, :]
            gs[h, at, :] = ref[512 + h * 128:640 + h * 128, :]
        qid[:, at] = ref[1280:1296, :]
    latents = jnp.concatenate([c[:, :512] for c in (c0, c1, c2, c3)], axis=0)
    keys = jnp.dot(latents, wk[...], preferred_element_type=F32).astype(BF)
    values = jnp.dot(latents, wv[...], preferred_element_type=F32).astype(BF)
    lane = lax.broadcasted_iota(jnp.int32, (128, 128), 1)
    for h in range(HEADS):
        kc[h, :, 0:128] = keys[:, h * 128:(h + 1) * 128]
        vs[h, :, :] = values[:, h * 128:(h + 1) * 128]
    q_marks = qid[0:1, :].astype(F32)
    q_pos = zi * QROWS + lax.broadcasted_iota(jnp.int32, (128, QROWS), 1)
    for j, c in enumerate((c0, c1, c2, c3)):
        tail = c[:, 512:640].astype(F32)
        even = jnp.where(lane < 64, tail, 0.0)
        odd = pltpu.roll(even, 64, 1)
        for h in range(HEADS):
            kc[h, j * 128:(j + 1) * 128, 128:256] = (odd if h % 2 else even).astype(BF)
        first = ((zi - j) & (Z - 1)) * QROWS + xi * 128
        k_pos = first + lax.broadcasted_iota(jnp.int32, (128, QROWS), 0)
        allowed = (k_pos <= q_pos) & (tail[:, 64:65] == q_marks)
        bias[j * 128:(j + 1) * 128, :] = jnp.where(allowed, 0.0, NEG)
    for h in range(HEADS):
        for b in range(0, QROWS, 256):
            sl = slice(b, b + 256)
            s = lax.dot_general(kc[h], qc[h, sl, :], NT, preferred_element_type=F32) * SCALE + bias[:, sl]
            dp = lax.dot_general(vs[h], gs[h, sl, :], NT, preferred_element_type=F32)
            m = jnp.max(s, axis=0, keepdims=True)
            e = jnp.exp(s - m)
            stats[h:h + 1, sl] = m
            stats[4 + h:5 + h, sl] = jnp.sum(e, axis=0, keepdims=True)
            stats[8 + h:9 + h, sl] = jnp.sum(e * dp, axis=0, keepdims=True)
    stats[12:16, :] = jnp.zeros((4, QROWS), F32)


def run_stats(where, qs, cs, wk, wv):
    sds = jax.ShapeDtypeStruct
    return call(
        stats_kernel,
        (sds((4, QROWS, 256), BF), sds((4, QROWS, 128), BF), sds((4, KROWS, 256), BF), sds((4, KROWS, 128), BF),
         sds((KROWS, QROWS), F32), sds((16, QROWS), F32)),
        1, 10, scratch=[pltpu.VMEM((16, QROWS), BF)], flops=1_400_000_000, nbytes=8 << 20,
    )(where, *qs, *cs, wk, wv)


def grads_kernel(where, t0, t1, t2, t3, qc, gs, kc, vs, bias, c0, c1, c2, c3, wk, wv,
                 w_keep, w_send, d0, d1, d2, d3, o0, o1, o2, o3, p_scr, s_scr, dkv, dq):
    xi, core = where[0], where[2]
    tops = [t[0:4, :] for t in (t0, t1, t2, t3)]
    top = functools.reduce(jnp.maximum, tops)
    total = jnp.zeros((4, QROWS), F32)
    cross = jnp.zeros((4, QROWS), F32)
    for t, m in zip((t0, t1, t2, t3), tops):
        f = jnp.exp(m - top)
        total = total + f * t[4:8, :]
        cross = cross + f * t[8:12, :]
    inv = 1.0 / total
    delta = cross * inv
    rope_grad = [jnp.zeros((KROWS, 128), F32), jnp.zeros((KROWS, 128), F32)]
    pair = None
    for h in range(HEADS):
        for b in range(0, QROWS, 256):
            sl = slice(b, b + 256)
            s = lax.dot_general(kc[h], qc[h, sl, :], NT, preferred_element_type=F32) * SCALE + bias[:, sl]
            dp = lax.dot_general(vs[h], gs[h, sl, :], NT, preferred_element_type=F32)
            p = jnp.exp(s - top[h:h + 1, sl]) * inv[h:h + 1, sl]
            p_scr[h % 2, :, sl] = p.astype(BF)
            s_scr[h % 2, :, sl] = (p * (dp - delta[h:h + 1, sl]) * SCALE).astype(BF)
        cols = slice(h * 128, (h + 1) * 128)
        dkv[1, :, cols] = jnp.dot(p_scr[h % 2], gs[h], preferred_element_type=F32).astype(BF)
        dk = jnp.dot(s_scr[h % 2], qc[h], preferred_element_type=F32)
        dkv[0, :, cols] = dk[:, :128].astype(BF)
        rope_grad[h % 2] = rope_grad[h % 2] + dk[:, 128:]
        dqh = lax.dot_general(s_scr[h % 2], kc[h], TN, preferred_element_type=F32)
        dq[:, cols] = dqh[:, :128].astype(BF)
        if h % 2 == 0:
            pair = dqh[:, 128:]
        else:
            dq[:, 512 + h // 2 * 128:640 + h // 2 * 128] = (pair + dqh[:, 128:]).astype(BF)
    latents = jnp.concatenate([c[:, :512] for c in (c0, c1, c2, c3)], axis=0)
    for out, which in ((w_send, 1 - core), (w_keep, core)):
        w = lax.dot_general(dkv[which], latents, TN, preferred_element_type=F32).astype(BF)
        for r in range(32):
            out[r % 4, r // 4 * 16:r // 4 * 16 + 16, :] = w[r * 16:r * 16 + 16, :]
    lat = (lax.dot_general(dkv[0], wk[...], NT, preferred_element_type=F32)
           + lax.dot_general(dkv[1], wv[...], NT, preferred_element_type=F32)).astype(BF)
    lane = lax.broadcasted_iota(jnp.int32, (KROWS, 128), 1)
    tail = jnp.where(lane < 64, rope_grad[0] + pltpu.roll(rope_grad[1], 64, 1), 0.0).astype(BF)
    for j, d in enumerate((d0, d1, d2, d3)):
        d[:, :512] = lat[j * 128:(j + 1) * 128, :]
        d[:, 512:640] = tail[j * 128:(j + 1) * 128, :]
    for s, o in enumerate((o0, o1, o2, o3)):
        o[...] = dq[pl.ds(pl.multiple_of(((xi + s) & 3) * 128, 128), 128), :]


def run_grads(where, ts, mats, cs, wk, wv):
    sds = jax.ShapeDtypeStruct
    return call(
        grads_kernel,
        tuple([sds((4, 128, 512), BF)] * 2 + [sds((128, 640), BF)] * 4 + [sds((128, 768), BF)] * 4),
        1, 4 + 5 + 4 + 2,
        scratch=[pltpu.VMEM((2, KROWS, QROWS), BF), pltpu.VMEM((2, KROWS, QROWS), BF),
                 pltpu.VMEM((2, KROWS, 512), BF), pltpu.VMEM((QROWS, 768), BF)],
        flops=3_000_000_000, nbytes=10 << 20,
    )(where, *ts, *mats, *cs, wk, wv)


def spread_kernel(where, keep, recv, o0, o1, o2, o3):
    xi = where[0]
    for s, o in enumerate((o0, o1, o2, o3)):
        at = (xi + s) & 3
        o[...] = (keep[at].astype(F32) + recv[at].astype(F32)).astype(BF)


def spread(where, keep, recv):
    return call(spread_kernel, tuple([jax.ShapeDtypeStruct((128, 512), BF)] * 4), 1, 2, nbytes=2 << 20)(where, keep, recv)


def wide_sum(*parts):
    return functools.reduce(jnp.add, [p.astype(F32) for p in parts])


def body(kv_latent, q_nope, q_rope, w_key_up, w_value_up, out_grad, segment_ids):
    ctx = lax.axis_index("ctx")
    dp = lax.axis_index("dp")
    core = dp % 2
    where = jnp.stack([ctx % X, ctx // X, core]).astype(jnp.int32)
    q, c = pack(q_nope[0], q_rope[0], out_grad[0], kv_latent[0], segment_ids)
    qs = (q, x_shift(q, -1), x_shift(q, 2), x_shift(q, 1))
    c1 = z_shift(c, 1)
    c2 = z_shift(c1, 1)
    c3 = z_shift(c2, 1)
    cs = (c, c1, c2, c3)
    *mats, stats = run_stats(where, qs, cs, w_key_up, w_value_up)
    ts = (stats, x_shift(stats, 1), x_shift(stats, 2), x_shift(stats, -1))
    w_keep, w_send, d0, d1, d2, d3, o0, o1, o2, o3 = run_grads(where, ts, mats, cs, w_key_up, w_value_up)
    pieces = spread(where, w_keep, core_swap(w_send))
    w = wide_sum(pieces[0], x_shift(pieces[1], 1), x_shift(pieces[2], 2), x_shift(pieces[3], -1)).astype(BF)
    w = lax.all_to_all(w, "ctx", 0, 0, tiled=True, axis_index_groups=[[z * X + x for z in range(Z)] for x in range(X)])
    w = jnp.sum(w.reshape(Z, 16, 512).astype(F32), axis=0).astype(BF)
    w = wide_sum(w, y_shift(w, 1), y_shift(w, 2), y_shift(w, -1))
    other = core_swap(w)
    grad_key = jnp.where(core == 0, w, other)
    grad_value = jnp.where(core == 0, other, w)
    d = z_shift(d3, -1)
    d = z_shift(wide_sum(d, d2).astype(BF), -1)
    d = z_shift(wide_sum(d, d1).astype(BF), -1)
    grad_latent = wide_sum(d, d0).astype(BF)[:, :576]
    grad_q = wide_sum(o0, x_shift(o1, 1), x_shift(o2, 2), x_shift(o3, -1)).astype(BF)
    return grad_q[None, :, :512], grad_q[None, :, 512:], grad_latent[None], grad_key, grad_value


def solution(mesh):
    return jax.shard_map(
        body,
        mesh=mesh,
        in_specs=(
            P("dp", "ctx", None),
            P("dp", "ctx", None),
            P("dp", "ctx", None),
            P(),
            P(),
            P("dp", "ctx", None),
            P("dp", "ctx"),
        ),
        out_specs=(
            P("dp", "ctx", None),
            P("dp", "ctx", None),
            P("dp", "ctx", None),
            P("ctx", None),
            P("ctx", None),
        ),
        check_vma=False,
    )
```

```python
import functools

import jax
import jax.numpy as jnp
from jax import lax
from jax.experimental import pallas as pl
from jax.experimental.pallas import tpu as pltpu
from jax.sharding import PartitionSpec as P

Z, X, Y = 8, 4, 4
HEADS, HEAD, ROPE, LATENT = 4, 128, 64, 512
ROWS = 128
REACH = 4
QROWS = X * ROWS
KROWS = REACH * ROWS
HALF = KROWS // 2
SCALE = (HEAD + ROPE) ** -0.5
NEG = -1e30
CUT = 640
PACK_VMEM = 60.5
BF, F32 = jnp.bfloat16, jnp.float32
NT = (((1,), (1,)), ((), ()))
TN = (((0,), (0,)), ((), ()))
VMEM = pl.BlockSpec(memory_space=pltpu.VMEM)
SMEM = pl.BlockSpec(memory_space=pltpu.SMEM)
HBM = pl.BlockSpec(memory_space=pltpu.HBM)


def x_shift(v, s):
    return lax.ppermute(v, "ctx", [(i, i // X * X + (i % X + s) % X) for i in range(Z * X)])


def z_shift(v, s):
    return lax.ppermute(v, "ctx", [(i, (i + s * X) % (Z * X)) for i in range(Z * X)])


def y_pair(v, far):
    pairs = [(i, 2 * ((Y - 1 - i // 2) if far else (i // 2 ^ 1)) + i % 2) for i in range(2 * Y)]
    return lax.ppermute(v, "dp", pairs)


def core_swap(v):
    return lax.ppermute(v, "dp", [(i, i ^ 1) for i in range(2 * Y)])


def call(kernel, out_shape, n_smem, n_vmem, n_hbm=0, scratch=(), flops=0, nbytes=0, vmem=16):
    return pl.pallas_call(
        kernel,
        out_shape=out_shape,
        in_specs=[SMEM] * n_smem + [VMEM] * n_vmem + [HBM] * n_hbm,
        out_specs=jax.tree.map(lambda _: VMEM, out_shape),
        scratch_shapes=list(scratch),
        compiler_params=pltpu.CompilerParams(vmem_limit_bytes=int(vmem * (1 << 20))),
        cost_estimate=pl.CostEstimate(flops=flops, bytes_accessed=nbytes, transcendentals=0),
    )


def pack_kernel(nope, rope, grad, kv_t, ids, q_out, ca_out, cb_out, kv_scr, ids_scr, sems):
    copies = [pltpu.make_async_copy(kv_t, kv_scr, sems.at[0]), pltpu.make_async_copy(ids, ids_scr, sems.at[1])]
    for n, (source, parts) in enumerate(((nope, 4), (grad, 4), (rope, 2))):
        for i in range(parts):
            at = n * 512 + i * 128
            copies.append(pltpu.make_async_copy(
                source.at[:, i * 128:(i + 1) * 128], q_out.at[at:at + 128, :], sems.at[len(copies)]))
    for copy in copies:
        copy.start()
    copies[0].wait()
    copies[1].wait()
    marks = jnp.broadcast_to(ids_scr[...].astype(F32), (128, 128)).astype(BF)
    q_out[1280:1296, :] = marks[:16]
    rows = jnp.concatenate([kv_scr[...], marks[:64]], axis=0).T
    ca_out[...] = rows[:64]
    cb_out[...] = rows[64:]
    for copy in copies[2:]:
        copy.wait()


def pack(nope, rope, grad, kv_t, ids):
    half = jax.ShapeDtypeStruct((64, 640), BF)
    return call(
        pack_kernel, (jax.ShapeDtypeStruct((1296, 128), BF), half, half), 0, 0, 5,
        scratch=[pltpu.VMEM((576, 128), BF), pltpu.VMEM((1, 128), jnp.int32), pltpu.SemaphoreType.DMA((12,))],
        nbytes=1 << 20, vmem=PACK_VMEM)(nope, rope, grad, kv_t, ids)


def keys_kernel(a0, a1, b0, b1, wk, wv, kc, vs, latents, marks, wk_out=None, wv_out=None):
    lane = lax.broadcasted_iota(jnp.int32, (64, 128), 1)
    for n, c in enumerate((a0, b0, a1, b1)):
        at = slice(n * 64, n * 64 + 64)
        latents[at, :] = c[:, :512]
        tail = c[:, 512:640].astype(F32)
        marks[at, :] = tail
        even = jnp.where(lane < 64, tail, 0.0)
        odd = pltpu.roll(even, 64, 1)
        for h in range(HEADS):
            kc[h, at, 128:256] = (odd if h % 2 else even).astype(BF)
    keys = jnp.dot(latents[...], wk[...], preferred_element_type=F32).astype(BF)
    values = jnp.dot(latents[...], wv[...], preferred_element_type=F32).astype(BF)
    for h in range(HEADS):
        kc[h, :, 0:128] = keys[:, h * 128:(h + 1) * 128]
        vs[h, :, :] = values[:, h * 128:(h + 1) * 128]
    if wk_out is not None:
        wk_out[...] = wk[...]
        wv_out[...] = wv[...]


def run_keys(ca, cb, wk, wv, hand_on):
    sds = jax.ShapeDtypeStruct
    return call(
        keys_kernel,
        (sds((4, HALF, 256), BF), sds((4, HALF, 128), BF), sds((HALF, LATENT), BF), sds((HALF, 128), F32),
         *([sds((512, 512), BF)] * (2 if hand_on else 0))),
        0, 6, flops=500_000_000, nbytes=2 << 20,
    )(*ca, *cb, wk, wv)


def stats_kernel(where, q0, q1, q2a, q2b, q3, kc0, kc1, vs0, vs1, marks0, marks1, qc, gs, es, dps, stats, bias, qid):
    xi, zi = where[0], where[1]
    for s, block in enumerate((q0, q1, (q2a, q2b), q3)):
        at = pl.ds(pl.multiple_of(((xi + s) & 3) * 128, 128), 128)

        def rows(first, count=128):
            if s != 2:
                return block[first:first + count, :]
            part, start = (block[1], first - CUT) if first >= CUT else (block[0], first)
            return part[start:start + count, :]

        for h in range(HEADS):
            qc[h, at, 0:128] = rows(h * 128)
            qc[h, at, 128:256] = rows(1024 + h // 2 * 128)
            gs[h, at, :] = rows(512 + h * 128)
        qid[:, at] = rows(1280, 16)
    q_marks = qid[0:1, :].astype(F32)
    q_pos = zi * QROWS + lax.broadcasted_iota(jnp.int32, (128, QROWS), 1)
    for j in range(REACH):
        at = slice(j * 128, j * 128 + 128)
        first = ((zi - j) & (Z - 1)) * QROWS + xi * 128
        k_pos = first + lax.broadcasted_iota(jnp.int32, (128, QROWS), 0)
        allowed = (k_pos <= q_pos) & ((marks0, marks1)[j // 2][j % 2 * 128:j % 2 * 128 + 128, 64:65] == q_marks)
        bias[at, :] = jnp.where(allowed, 0.0, NEG)
    for h in range(HEADS):
        for b in range(0, QROWS, 256):
            sl = slice(b, b + 256)
            parts = []
            for n, (kc, vs) in enumerate(((kc0, vs0), (kc1, vs1))):
                at = slice(n * HALF, (n + 1) * HALF)
                s = lax.dot_general(kc[h], qc[h, sl, :], NT, preferred_element_type=F32) * SCALE + bias[at, sl]
                dp = lax.dot_general(vs[h], gs[h, sl, :], NT, preferred_element_type=F32)
                dps[h, at, sl] = dp
                parts.append((at, s, dp))
            m = jnp.maximum(*[jnp.max(s, axis=0, keepdims=True) for _, s, _ in parts])
            total = cross = 0.0
            for at, s, dp in parts:
                e = jnp.exp(s - m)
                es[h, at, sl] = e
                total = total + jnp.sum(e, axis=0, keepdims=True)
                cross = cross + jnp.sum(e * dp, axis=0, keepdims=True)
            stats[h:h + 1, sl] = m
            stats[4 + h:5 + h, sl] = total
            stats[8 + h:9 + h, sl] = cross
    stats[12:16, :] = jnp.zeros((4, QROWS), F32)


def run_stats(where, qs, *keys):
    sds = jax.ShapeDtypeStruct
    return call(
        stats_kernel,
        (sds((4, QROWS, 256), BF), sds((4, QROWS, 128), BF),
         sds((4, KROWS, QROWS), F32), sds((4, KROWS, QROWS), F32), sds((16, QROWS), F32)),
        1, 11, scratch=[pltpu.VMEM((KROWS, QROWS), F32), pltpu.VMEM((16, QROWS), BF)],
        flops=1_000_000_000, nbytes=8 << 20,
    )(where, *qs, *keys)


def weight_kernel(where, t0, t1, t2, t3, qc, gs, es, dps, latents0, latents1, wk, wv, w_keep, w_send, ds, dkv, tail, d3, p_scr):
    core = where[2]
    tops = [t[0:4, :] for t in (t0, t1, t2, t3)]
    top = functools.reduce(jnp.maximum, tops)
    total = jnp.zeros((4, QROWS), F32)
    cross = jnp.zeros((4, QROWS), F32)
    for t, m in zip((t0, t1, t2, t3), tops):
        f = jnp.exp(m - top)
        total = total + f * t[4:8, :]
        cross = cross + f * t[8:12, :]
    inv = 1.0 / total
    delta = cross * inv
    scaled = jnp.exp(tops[0] - top) * inv
    rope_grad = [jnp.zeros((KROWS, 128), F32), jnp.zeros((KROWS, 128), F32)]
    for h in range(HEADS):
        for b in range(0, QROWS, 256):
            sl = slice(b, b + 256)
            p = es[h, :, sl] * scaled[h:h + 1, sl]
            p_scr[h % 2, :, sl] = p.astype(BF)
            ds[h, :, sl] = (p * (dps[h, :, sl] - delta[h:h + 1, sl]) * SCALE).astype(BF)
        cols = slice(h * 128, (h + 1) * 128)
        dkv[1, :, cols] = jnp.dot(p_scr[h % 2], gs[h], preferred_element_type=F32).astype(BF)
        dk = jnp.dot(ds[h], qc[h], preferred_element_type=F32)
        dkv[0, :, cols] = dk[:, :128].astype(BF)
        rope_grad[h % 2] = rope_grad[h % 2] + dk[:, 128:]
    for out, which in ((w_send, 1 - core), (w_keep, core)):
        w = (lax.dot_general(dkv[which, :HALF], latents0[...], TN, preferred_element_type=F32)
             + lax.dot_general(dkv[which, HALF:], latents1[...], TN, preferred_element_type=F32)).astype(BF)
        for r in range(32):
            out[r % 4, r // 4 * 16:r // 4 * 16 + 16, :] = w[r * 16:r * 16 + 16, :]
    lane = lax.broadcasted_iota(jnp.int32, (KROWS, 128), 1)
    tail[...] = jnp.where(lane < 64, rope_grad[0] + pltpu.roll(rope_grad[1], 64, 1), 0.0).astype(BF)
    far = slice(3 * ROWS, KROWS)
    d3[:, :512] = (lax.dot_general(dkv[0, far], wk[...], NT, preferred_element_type=F32)
                   + lax.dot_general(dkv[1, far], wv[...], NT, preferred_element_type=F32)).astype(BF)
    d3[:, 512:640] = tail[far, :]


def run_weight(where, ts, *mats):
    sds = jax.ShapeDtypeStruct
    return call(
        weight_kernel,
        (sds((4, 128, 512), BF), sds((4, 128, 512), BF), sds((4, KROWS, QROWS), BF), sds((2, KROWS, 512), BF),
         sds((KROWS, 128), BF), sds((128, 640), BF)),
        1, 12, scratch=[pltpu.VMEM((2, KROWS, QROWS), BF)], flops=1_500_000_000, nbytes=10 << 20,
    )(where, *ts, *mats)


def grads_kernel(where, ds, dkv, tail, kc0, kc1, wk, wv, d0, d1, d2, o0, o1, o2, o3, dq):
    xi = where[0]
    near = slice(0, 3 * ROWS)
    lat = (lax.dot_general(dkv[0, near], wk[...], NT, preferred_element_type=F32)
           + lax.dot_general(dkv[1, near], wv[...], NT, preferred_element_type=F32)).astype(BF)
    for j, d in enumerate((d0, d1, d2)):
        d[:, :512] = lat[j * 128:(j + 1) * 128, :]
        d[:, 512:640] = tail[j * 128:(j + 1) * 128, :]
    for p in range(2):
        pair = 0.0
        for h in (2 * p, 2 * p + 1):
            dqh = (lax.dot_general(ds[h, :HALF], kc0[h], TN, preferred_element_type=F32)
                   + lax.dot_general(ds[h, HALF:], kc1[h], TN, preferred_element_type=F32))
            dq[:, h * 128:(h + 1) * 128] = dqh[:, :128].astype(BF)
            pair = pair + dqh[:, 128:]
        dq[:, 512 + p * 128:640 + p * 128] = pair.astype(BF)
    for s, o in enumerate((o0, o1, o2, o3)):
        o[...] = dq[pl.ds(pl.multiple_of(((xi + s) & 3) * 128, 128), 128), :]


def run_grads(where, ds, dkv, tail, kc0, kc1, wk, wv):
    sds = jax.ShapeDtypeStruct
    return call(
        grads_kernel,
        tuple([sds((128, 640), BF)] * 3 + [sds((128, 768), BF)] * 4),
        1, 7, scratch=[pltpu.VMEM((QROWS, 768), BF)], flops=1_500_000_000, nbytes=10 << 20,
    )(where, ds, dkv, tail, kc0, kc1, wk, wv)


def spread_kernel(where, keep, recv, o0, o1, o2, o3):
    xi = where[0]
    for s, o in enumerate((o0, o1, o2, o3)):
        at = (xi + s) & 3
        o[...] = (keep[at].astype(F32) + recv[at].astype(F32)).astype(BF)


def spread(where, keep, recv):
    return call(spread_kernel, tuple([jax.ShapeDtypeStruct((128, 512), BF)] * 4), 1, 2, nbytes=2 << 20)(where, keep, recv)


def wide(*refs):
    return functools.reduce(jnp.add, [r[...].astype(F32) for r in refs])


def sum_kernel(*refs):
    refs[-1][...] = wide(*refs[:-1]).astype(refs[-1].dtype)


def add_up(*parts, dtype=BF):
    return call(sum_kernel, jax.ShapeDtypeStruct(parts[0].shape, dtype), 0, len(parts), nbytes=1 << 20)(*parts)


def sum_z_kernel(parts, w):
    w[...] = jnp.sum(parts[...].reshape(Z, 16, 512).astype(F32), axis=0).astype(BF)


def query_kernel(q0, q1, q2, q3, nope, rope):
    q = wide(q0, q1, q2, q3).astype(BF)
    nope[...] = q[:, :512]
    rope[...] = q[:, 512:]


def latent_kernel(d1, d0, latent):
    latent[...] = wide(d1, d0).astype(BF)[:, :576].T


def body(kv_latent, q_nope, q_rope, w_key_up, w_value_up, out_grad, segment_ids):
    ctx = lax.axis_index("ctx")
    dp = lax.axis_index("dp")
    core = dp % 2
    where = jnp.stack([ctx % X, ctx // X, core]).astype(jnp.int32)
    q, ca, cb = pack(q_nope[0], q_rope[0], out_grad[0], kv_latent[0].T, segment_ids)
    ca, cb = [ca], [cb]
    for _ in range(REACH - 1):
        ca.append(z_shift(ca[-1], 1))
        cb.append(z_shift(cb[-1], 1))
    right, left = x_shift(q, -1), x_shift(q, 1)
    qs = (q, right, x_shift(left[:CUT], 1), x_shift(right[CUT:], -1), left)
    kc0, vs0, latents0, marks0, wk, wv = run_keys(ca[:2], cb[:2], w_key_up, w_value_up, True)
    kc1, vs1, latents1, marks1 = run_keys(ca[2:], cb[2:], wk, wv, False)
    qc, gs, es, dps, stats = run_stats(where, qs, kc0, kc1, vs0, vs1, marks0, marks1)
    ts = (stats, x_shift(stats, 1), x_shift(stats, 2), x_shift(stats, -1))
    w_keep, w_send, ds, dkv, tail, d3 = run_weight(where, ts, qc, gs, es, dps, latents0, latents1, wk, wv)
    received = core_swap(w_send)
    d0, d1, d2, o0, o1, o2, o3 = run_grads(where, ds, dkv, tail, kc0, kc1, wk, wv)
    pieces = spread(where, w_keep, received)
    sds = jax.ShapeDtypeStruct
    w = add_up(pieces[0], x_shift(pieces[1], 1), x_shift(pieces[2], 2), x_shift(pieces[3], -1))
    w = lax.all_to_all(w, "ctx", 0, 0, tiled=True, axis_index_groups=[[z * X + x for z in range(Z)] for x in range(X)])
    w = call(sum_z_kernel, sds((16, 512), BF), 0, 1, nbytes=1 << 18)(w)
    w = add_up(w, y_pair(w, False))
    w = add_up(w, y_pair(w, True), dtype=F32)
    other = core_swap(w)
    grad_key = jnp.where(core == 0, w, other)
    grad_value = jnp.where(core == 0, other, w)
    d = add_up(z_shift(d3, -1), d2)
    d = add_up(z_shift(d, -1), d1)
    grad_latent = call(latent_kernel, sds((576, 128), BF), 0, 2, nbytes=1 << 20)(z_shift(d, -1), d0)
    grad_nope, grad_rope = call(query_kernel, (sds((128, 512), BF), sds((128, 256), BF)), 0, 4, nbytes=1 << 20)(
        o0, x_shift(o1, 1), x_shift(o2, 2), x_shift(o3, -1))
    return grad_nope[None], grad_rope[None], grad_latent.T[None], grad_key, grad_value


def solution(mesh):
    return jax.shard_map(
        body,
        mesh=mesh,
        in_specs=(
            P("dp", "ctx", None),
            P("dp", "ctx", None),
            P("dp", "ctx", None),
            P(),
            P(),
            P("dp", "ctx", None),
            P("dp", "ctx"),
        ),
        out_specs=(
            P("dp", "ctx", None),
            P("dp", "ctx", None),
            P("dp", "ctx", None),
            P("ctx", None),
            P("ctx", None),
        ),
        check_vma=False,
    )
```

```python
import functools

import jax
import jax.numpy as jnp
from jax import lax
from jax.experimental import pallas as pl
from jax.experimental.pallas import tpu as pltpu
from jax.sharding import PartitionSpec as P

Z, X, Y = 8, 4, 4
HEADS, HEAD, ROPE, LATENT = 4, 128, 64, 512
ROWS = 128
REACH = 4
QROWS = X * ROWS
KROWS = REACH * ROWS
HALF = KROWS // 2
ORDER = (1, 2, 0, 3)
SCALE = (HEAD + ROPE) ** -0.5
NEG = -1e30
CUTS = (64, 64)
PACK_VMEM = 60.5
BF, F32 = jnp.bfloat16, jnp.float32
NT = (((1,), (1,)), ((), ()))
TN = (((0,), (0,)), ((), ()))
VMEM = pl.BlockSpec(memory_space=pltpu.VMEM)
SMEM = pl.BlockSpec(memory_space=pltpu.SMEM)
HBM = pl.BlockSpec(memory_space=pltpu.HBM)


def x_shift(v, s):
    return lax.ppermute(v, "ctx", [(i, i // X * X + (i % X + s) % X) for i in range(Z * X)])


def z_shift(v, s):
    return lax.ppermute(v, "ctx", [(i, (i + s * X) % (Z * X)) for i in range(Z * X)])


def y_pair(v, far):
    pairs = [(i, 2 * ((Y - 1 - i // 2) if far else (i // 2 ^ 1)) + i % 2) for i in range(2 * Y)]
    return lax.ppermute(v, "dp", pairs)


def core_swap(v):
    return lax.ppermute(v, "dp", [(i, i ^ 1) for i in range(2 * Y)])


def call(kernel, out_shape, n_smem, n_vmem, n_hbm=0, scratch=(), flops=0, nbytes=0, vmem=16):
    return pl.pallas_call(
        kernel,
        out_shape=out_shape,
        in_specs=[SMEM] * n_smem + [VMEM] * n_vmem + [HBM] * n_hbm,
        out_specs=jax.tree.map(lambda _: VMEM, out_shape),
        scratch_shapes=list(scratch),
        compiler_params=pltpu.CompilerParams(vmem_limit_bytes=int(vmem * (1 << 20))),
        cost_estimate=pl.CostEstimate(flops=flops, bytes_accessed=nbytes, transcendentals=0),
    )


def pack_kernel(nope, rope, grad, kv_t, ids, q_out, *rest):
    *c_outs, kv_scr, ids_scr, sems = rest
    copies = [pltpu.make_async_copy(kv_t, kv_scr, sems.at[0]), pltpu.make_async_copy(ids, ids_scr, sems.at[1])]
    for n, (source, parts) in enumerate(((nope, 4), (grad, 4), (rope, 2))):
        for i in range(parts):
            at = n * 512 + i * 128
            copies.append(pltpu.make_async_copy(
                source.at[:, i * 128:(i + 1) * 128], q_out.at[at:at + 128, :], sems.at[len(copies)]))
    for copy in copies:
        copy.start()
    copies[0].wait()
    copies[1].wait()
    marks = jnp.broadcast_to(ids_scr[...].astype(F32), (128, 128)).astype(BF)
    q_out[1280:1296, :] = marks[:16]
    rows = jnp.concatenate([kv_scr[...], marks[:64]], axis=0).T
    first = 0
    for c_out in c_outs:
        c_out[...] = rows[first:first + c_out.shape[0]]
        first += c_out.shape[0]
    for copy in copies[2:]:
        copy.wait()


def pack(nope, rope, grad, kv_t, ids):
    pieces = [jax.ShapeDtypeStruct((rows, 640), BF) for rows in CUTS]
    return call(
        pack_kernel, (jax.ShapeDtypeStruct((1296, 128), BF), *pieces), 0, 0, 5,
        scratch=[pltpu.VMEM((576, 128), BF), pltpu.VMEM((1, 128), jnp.int32), pltpu.SemaphoreType.DMA((12,))],
        nbytes=1 << 20, vmem=PACK_VMEM)(nope, rope, grad, kv_t, ids)


def open_kernel(*refs):
    pieces, (latents, ropes, marks) = refs[:-3], refs[-3:]
    first = 0
    for c in pieces:
        at = slice(first, first + c.shape[0])
        first += c.shape[0]
        latents[at, :] = c[:, :512]
        tail = c[:, 512:640].astype(F32)
        marks[at, :] = tail
        even = jnp.where(lax.broadcasted_iota(jnp.int32, tail.shape, 1) < 64, tail, 0.0)
        ropes[0, at, :] = even.astype(BF)
        ropes[1, at, :] = pltpu.roll(even, 64, 1).astype(BF)


def keys_kernel(latents, ropes, wk, wv, kc, vs, *weights):
    keys = jnp.dot(latents[...], wk[...], preferred_element_type=F32).astype(BF)
    values = jnp.dot(latents[...], wv[...], preferred_element_type=F32).astype(BF)
    for h in range(HEADS):
        kc[h, :, 0:128] = keys[:, h * 128:(h + 1) * 128]
        kc[h, :, 128:256] = ropes[h % 2]
        vs[h, :, :] = values[:, h * 128:(h + 1) * 128]
    for out, w in zip(weights, (wk, wv)):
        out[...] = w[...]


def run_keys(pieces, wk, wv, hand_on):
    sds = jax.ShapeDtypeStruct
    latents, ropes, marks = call(
        open_kernel, (sds((HALF, LATENT), BF), sds((2, HALF, 128), BF), sds((HALF, 128), F32)),
        0, len(pieces), flops=1_500_000_000, nbytes=1 << 20)(*pieces)
    kc, vs, *weights = call(
        keys_kernel,
        (sds((4, HALF, 256), BF), sds((4, HALF, 128), BF), *([sds((512, 512), BF)] * (2 if hand_on else 0))),
        0, 4, flops=500_000_000, nbytes=2 << 20)(latents, ropes, wk, wv)
    return kc, vs, latents, marks, *weights


def stats_kernel(where, q0, q1, q2, q3, kc0, kc1, vs0, vs1, marks0, marks1, qc, gs, es, dps, stats, bias, qid):
    xi, zi = where[0], where[1]
    for s, block in enumerate((q0, q1, q2, q3)):
        at = pl.ds(pl.multiple_of(((xi + s) & 3) * 128, 128), 128)

        def rows(first, count=128):
            return block[first:first + count, :]

        for h in range(HEADS):
            qc[h, at, 0:128] = rows(h * 128)
            qc[h, at, 128:256] = rows(1024 + h // 2 * 128)
            gs[h, at, :] = rows(512 + h * 128)
        qid[:, at] = rows(1280, 16)
    q_marks = qid[0:1, :].astype(F32)
    q_pos = zi * QROWS + lax.broadcasted_iota(jnp.int32, (128, QROWS), 1)
    for j in range(REACH):
        at = slice(j * 128, j * 128 + 128)
        first = ((zi - ORDER[j]) & (Z - 1)) * QROWS + xi * 128
        k_pos = first + lax.broadcasted_iota(jnp.int32, (128, QROWS), 0)
        allowed = (k_pos <= q_pos) & ((marks0, marks1)[j // 2][j % 2 * 128:j % 2 * 128 + 128, 64:65] == q_marks)
        bias[at, :] = jnp.where(allowed, 0.0, NEG)
    for h in range(HEADS):
        for b in range(0, QROWS, 256):
            sl = slice(b, b + 256)
            parts = []
            for n, (kc, vs) in enumerate(((kc0, vs0), (kc1, vs1))):
                at = slice(n * HALF, (n + 1) * HALF)
                s = lax.dot_general(kc[h], qc[h, sl, :], NT, preferred_element_type=F32) * SCALE + bias[at, sl]
                dp = lax.dot_general(vs[h], gs[h, sl, :], NT, preferred_element_type=F32)
                dps[h, at, sl] = dp
                parts.append((at, s, dp))
            m = jnp.maximum(*[jnp.max(s, axis=0, keepdims=True) for _, s, _ in parts])
            total = cross = 0.0
            for at, s, dp in parts:
                e = jnp.exp(s - m)
                es[h, at, sl] = e
                total = total + jnp.sum(e, axis=0, keepdims=True)
                cross = cross + jnp.sum(e * dp, axis=0, keepdims=True)
            stats[h:h + 1, sl] = m
            stats[4 + h:5 + h, sl] = total
            stats[8 + h:9 + h, sl] = cross
    stats[12:16, :] = jnp.zeros((4, QROWS), F32)


def run_stats(where, qs, *keys):
    sds = jax.ShapeDtypeStruct
    return call(
        stats_kernel,
        (sds((4, QROWS, 256), BF), sds((4, QROWS, 128), BF),
         sds((4, KROWS, QROWS), F32), sds((4, KROWS, QROWS), F32), sds((16, QROWS), F32)),
        1, 10, scratch=[pltpu.VMEM((KROWS, QROWS), F32), pltpu.VMEM((16, QROWS), BF)],
        flops=1_000_000_000, nbytes=8 << 20,
    )(where, *qs, *keys)


def weight_kernel(where, t0, t1, t2, t3, qc, gs, es, dps, latents0, latents1, wk, wv, w_keep, w_send, ds, dkv, tail, d3, p_scr):
    core = where[2]
    tops = [t[0:4, :] for t in (t0, t1, t2, t3)]
    top = functools.reduce(jnp.maximum, tops)
    total = jnp.zeros((4, QROWS), F32)
    cross = jnp.zeros((4, QROWS), F32)
    for t, m in zip((t0, t1, t2, t3), tops):
        f = jnp.exp(m - top)
        total = total + f * t[4:8, :]
        cross = cross + f * t[8:12, :]
    inv = 1.0 / total
    delta = cross * inv
    scaled = jnp.exp(tops[0] - top) * inv
    rope_grad = [jnp.zeros((KROWS, 128), F32), jnp.zeros((KROWS, 128), F32)]
    for h in range(HEADS):
        for b in range(0, QROWS, 256):
            sl = slice(b, b + 256)
            p = es[h, :, sl] * scaled[h:h + 1, sl]
            p_scr[h % 2, :, sl] = p.astype(BF)
            ds[h, :, sl] = (p * (dps[h, :, sl] - delta[h:h + 1, sl]) * SCALE).astype(BF)
        cols = slice(h * 128, (h + 1) * 128)
        dkv[1, :, cols] = jnp.dot(p_scr[h % 2], gs[h], preferred_element_type=F32).astype(BF)
        dk = jnp.dot(ds[h], qc[h], preferred_element_type=F32)
        dkv[0, :, cols] = dk[:, :128].astype(BF)
        rope_grad[h % 2] = rope_grad[h % 2] + dk[:, 128:]
    for out, which in ((w_send, 1 - core), (w_keep, core)):
        w = (lax.dot_general(dkv[which, :HALF], latents0[...], TN, preferred_element_type=F32)
             + lax.dot_general(dkv[which, HALF:], latents1[...], TN, preferred_element_type=F32)).astype(BF)
        for r in range(32):
            out[r % 4, r // 4 * 16:r // 4 * 16 + 16, :] = w[r * 16:r * 16 + 16, :]
    lane = lax.broadcasted_iota(jnp.int32, (KROWS, 128), 1)
    tail[...] = jnp.where(lane < 64, rope_grad[0] + pltpu.roll(rope_grad[1], 64, 1), 0.0).astype(BF)
    far = slice(3 * ROWS, KROWS)
    d3[:, :512] = (lax.dot_general(dkv[0, far], wk[...], NT, preferred_element_type=F32)
                   + lax.dot_general(dkv[1, far], wv[...], NT, preferred_element_type=F32)).astype(BF)
    d3[:, 512:640] = tail[far, :]


def run_weight(where, ts, *mats):
    sds = jax.ShapeDtypeStruct
    return call(
        weight_kernel,
        (sds((4, 128, 512), BF), sds((4, 128, 512), BF), sds((4, KROWS, QROWS), BF), sds((2, KROWS, 512), BF),
         sds((KROWS, 128), BF), sds((128, 640), BF)),
        1, 12, scratch=[pltpu.VMEM((2, KROWS, QROWS), BF)], flops=1_500_000_000, nbytes=10 << 20,
    )(where, *ts, *mats)


def grads_kernel(where, ds, dkv, tail, kc0, kc1, wk, wv, d0, d1, d2, o0, o1, o2, o3, dq):
    xi = where[0]
    near = slice(0, 3 * ROWS)
    lat = (lax.dot_general(dkv[0, near], wk[...], NT, preferred_element_type=F32)
           + lax.dot_general(dkv[1, near], wv[...], NT, preferred_element_type=F32)).astype(BF)
    for j, d in enumerate((d1, d2, d0)):
        d[:, :512] = lat[j * 128:(j + 1) * 128, :]
        d[:, 512:640] = tail[j * 128:(j + 1) * 128, :]
    for p in range(2):
        pair = 0.0
        for h in (2 * p, 2 * p + 1):
            dqh = (lax.dot_general(ds[h, :HALF], kc0[h], TN, preferred_element_type=F32)
                   + lax.dot_general(ds[h, HALF:], kc1[h], TN, preferred_element_type=F32))
            dq[:, h * 128:(h + 1) * 128] = dqh[:, :128].astype(BF)
            pair = pair + dqh[:, 128:]
        dq[:, 512 + p * 128:640 + p * 128] = pair.astype(BF)
    for s, o in enumerate((o0, o1, o2, o3)):
        o[...] = dq[pl.ds(pl.multiple_of(((xi + s) & 3) * 128, 128), 128), :]


def run_grads(where, ds, dkv, tail, kc0, kc1, wk, wv):
    sds = jax.ShapeDtypeStruct
    return call(
        grads_kernel,
        tuple([sds((128, 640), BF)] * 3 + [sds((128, 768), BF)] * 4),
        1, 7, scratch=[pltpu.VMEM((QROWS, 768), BF)], flops=1_500_000_000, nbytes=10 << 20,
    )(where, ds, dkv, tail, kc0, kc1, wk, wv)


def spread_kernel(where, keep, recv, o0, o1, o2, o3):
    xi = where[0]
    for s, o in enumerate((o0, o1, o2, o3)):
        at = (xi + s) & 3
        o[...] = (keep[at].astype(F32) + recv[at].astype(F32)).astype(BF)


def spread(where, keep, recv):
    return call(spread_kernel, tuple([jax.ShapeDtypeStruct((128, 512), BF)] * 4), 1, 2, nbytes=2 << 20)(where, keep, recv)


def wide(*refs):
    return functools.reduce(jnp.add, [r[...].astype(F32) for r in refs])


def sum_kernel(*refs):
    refs[-1][...] = wide(*refs[:-1]).astype(refs[-1].dtype)


def add_up(*parts, dtype=BF):
    return call(sum_kernel, jax.ShapeDtypeStruct(parts[0].shape, dtype), 0, len(parts), nbytes=1 << 20)(*parts)


def sum_z_kernel(parts, w):
    w[...] = jnp.sum(parts[...].reshape(Z, 16, 512).astype(F32), axis=0).astype(BF)


def query_kernel(q0, q1, q2, q3, nope, rope):
    q = wide(q0, q1, q2, q3).astype(BF)
    nope[...] = q[:, :512]
    rope[...] = q[:, 512:]


def latent_kernel(d2, d1, d0, latent):
    latent[...] = wide(d2, d1, d0).astype(BF)[:, :576].T


def body(kv_latent, q_nope, q_rope, w_key_up, w_value_up, out_grad, segment_ids):
    ctx = lax.axis_index("ctx")
    dp = lax.axis_index("dp")
    core = dp % 2
    where = jnp.stack([ctx % X, ctx // X, core]).astype(jnp.int32)
    q, *c = pack(q_nope[0], q_rope[0], out_grad[0], kv_latent[0].T, segment_ids)
    c1 = [z_shift(v, 1) for v in c]
    c2 = [z_shift(v, 1) for v in c1]
    kc0, vs0, latents0, marks0, wk, wv = run_keys(c1 + c2, w_key_up, w_value_up, True)
    c3 = [z_shift(v, 1) for v in c2]
    later, _ = lax.optimization_barrier((q, c1))
    qs = (q, x_shift(q, -1), x_shift(q, 2), x_shift(later, 1))
    kc1, vs1, latents1, marks1 = run_keys(c + c3, wk, wv, False)
    qc, gs, es, dps, stats = run_stats(where, qs, kc0, kc1, vs0, vs1, marks0, marks1)
    ts = (stats, x_shift(stats, 1), x_shift(stats, 2), x_shift(stats, -1))
    w_keep, w_send, ds, dkv, tail, d3 = run_weight(where, ts, qc, gs, es, dps, latents0, latents1, wk, wv)
    received = core_swap(w_send)
    d0, d1, d2, o0, o1, o2, o3 = run_grads(where, ds, dkv, tail, kc0, kc1, wk, wv)
    pieces = spread(where, w_keep, received)
    sds = jax.ShapeDtypeStruct
    w = add_up(pieces[0], x_shift(pieces[1], 1), x_shift(pieces[2], 2), x_shift(pieces[3], -1))
    w = lax.all_to_all(w, "ctx", 0, 0, tiled=True, axis_index_groups=[[z * X + x for z in range(Z)] for x in range(X)])
    d = add_up(z_shift(d3, -1), d2)
    grad_latent = call(latent_kernel, sds((576, 128), BF), 0, 3, flops=1_000_000_000, nbytes=1 << 20)(
        z_shift(d, -2), z_shift(d1, -1), d0)
    w, grad_latent = lax.optimization_barrier((w, grad_latent))
    w = call(sum_z_kernel, sds((16, 512), BF), 0, 1, nbytes=1 << 18)(w)
    w = add_up(w, y_pair(w, False))
    w = add_up(w, y_pair(w, True), dtype=F32)
    other = core_swap(w)
    grad_key = jnp.where(core == 0, w, other)
    grad_value = jnp.where(core == 0, other, w)
    grad_nope, grad_rope = call(query_kernel, (sds((128, 512), BF), sds((128, 256), BF)), 0, 4, nbytes=1 << 20)(
        o0, x_shift(o1, 1), x_shift(o2, 2), x_shift(o3, -1))
    return grad_nope[None], grad_rope[None], grad_latent.T[None], grad_key, grad_value


def solution(mesh):
    return jax.shard_map(
        body,
        mesh=mesh,
        in_specs=(
            P("dp", "ctx", None),
            P("dp", "ctx", None),
            P("dp", "ctx", None),
            P(),
            P(),
            P("dp", "ctx", None),
            P("dp", "ctx"),
        ),
        out_specs=(
            P("dp", "ctx", None),
            P("dp", "ctx", None),
            P("dp", "ctx", None),
            P("ctx", None),
            P("ctx", None),
        ),
        check_vma=False,
    )
```

```python
import functools

import jax
import jax.numpy as jnp
from jax import lax
from jax.experimental import pallas as pl
from jax.experimental.pallas import tpu as pltpu
from jax.sharding import PartitionSpec as P

Z, X, Y = 8, 4, 4
HEADS, HEAD, ROPE, LATENT = 4, 128, 64, 512
ROWS = 128
REACH = 4
QROWS = X * ROWS
KROWS = REACH * ROWS
HALF = KROWS // 2
ORDER = (1, 2, 0, 3)
SCALE = (HEAD + ROPE) ** -0.5
NEG = -1e30
CUTS = (64, 64)
PACK_VMEM = 60.5
BF, F32 = jnp.bfloat16, jnp.float32
NT = (((1,), (1,)), ((), ()))
TN = (((0,), (0,)), ((), ()))
VMEM = pl.BlockSpec(memory_space=pltpu.VMEM)
SMEM = pl.BlockSpec(memory_space=pltpu.SMEM)
HBM = pl.BlockSpec(memory_space=pltpu.HBM)


def x_shift(v, s):
    return lax.ppermute(v, "ctx", [(i, i // X * X + (i % X + s) % X) for i in range(Z * X)])


def z_shift(v, s):
    return lax.ppermute(v, "ctx", [(i, (i + s * X) % (Z * X)) for i in range(Z * X)])


def y_pair(v, far):
    pairs = [(i, 2 * ((Y - 1 - i // 2) if far else (i // 2 ^ 1)) + i % 2) for i in range(2 * Y)]
    return lax.ppermute(v, "dp", pairs)


def core_swap(v):
    return lax.ppermute(v, "dp", [(i, i ^ 1) for i in range(2 * Y)])


def call(kernel, out_shape, n_smem, n_vmem, n_hbm=0, scratch=(), flops=0, nbytes=0, vmem=16):
    return pl.pallas_call(
        kernel,
        out_shape=out_shape,
        in_specs=[SMEM] * n_smem + [VMEM] * n_vmem + [HBM] * n_hbm,
        out_specs=jax.tree.map(lambda _: VMEM, out_shape),
        scratch_shapes=list(scratch),
        compiler_params=pltpu.CompilerParams(vmem_limit_bytes=int(vmem * (1 << 20))),
        cost_estimate=pl.CostEstimate(flops=flops, bytes_accessed=nbytes, transcendentals=0),
    )


def pack_kernel(nope, rope, grad, kv_t, ids, q_out, *rest):
    *c_outs, kv_scr, ids_scr, sems = rest
    copies = [pltpu.make_async_copy(kv_t, kv_scr, sems.at[0]), pltpu.make_async_copy(ids, ids_scr, sems.at[1])]
    for n, (source, parts) in enumerate(((nope, 4), (grad, 4), (rope, 2))):
        for i in range(parts):
            at = n * 512 + i * 128
            copies.append(pltpu.make_async_copy(
                source.at[:, i * 128:(i + 1) * 128], q_out.at[at:at + 128, :], sems.at[len(copies)]))
    for copy in copies:
        copy.start()
    copies[0].wait()
    copies[1].wait()
    marks = jnp.broadcast_to(ids_scr[...].astype(F32), (128, 128)).astype(BF)
    q_out[1280:1296, :] = marks[:16]
    rows = jnp.concatenate([kv_scr[...], marks[:64]], axis=0).T
    first = 0
    for c_out in c_outs:
        c_out[...] = rows[first:first + c_out.shape[0]]
        first += c_out.shape[0]
    for copy in copies[2:]:
        copy.wait()


def pack(nope, rope, grad, kv_t, ids):
    pieces = [jax.ShapeDtypeStruct((rows, 640), BF) for rows in CUTS]
    return call(
        pack_kernel, (jax.ShapeDtypeStruct((1296, 128), BF), *pieces), 0, 0, 5,
        scratch=[pltpu.VMEM((576, 128), BF), pltpu.VMEM((1, 128), jnp.int32), pltpu.SemaphoreType.DMA((12,))],
        nbytes=1 << 20, vmem=PACK_VMEM)(nope, rope, grad, kv_t, ids)


def open_kernel(*refs):
    pieces, (latents, ropes, marks) = refs[:-3], refs[-3:]
    first = 0
    for c in pieces:
        at = slice(first, first + c.shape[0])
        first += c.shape[0]
        latents[at, :] = c[:, :512]
        tail = c[:, 512:640].astype(F32)
        marks[at, :] = tail
        even = jnp.where(lax.broadcasted_iota(jnp.int32, tail.shape, 1) < 64, tail, 0.0)
        ropes[0, at, :] = even.astype(BF)
        ropes[1, at, :] = pltpu.roll(even, 64, 1).astype(BF)


def keys_kernel(latents, ropes, wk, wv, kc, vs, *weights):
    keys = jnp.dot(latents[...], wk[...], preferred_element_type=F32).astype(BF)
    values = jnp.dot(latents[...], wv[...], preferred_element_type=F32).astype(BF)
    for h in range(HEADS):
        kc[h, :, 0:128] = keys[:, h * 128:(h + 1) * 128]
        kc[h, :, 128:256] = ropes[h % 2]
        vs[h, :, :] = values[:, h * 128:(h + 1) * 128]
    for out, w in zip(weights, (wk, wv)):
        out[...] = w[...]


def run_keys(pieces, wk, wv, hand_on):
    sds = jax.ShapeDtypeStruct
    latents, ropes, marks = call(
        open_kernel, (sds((HALF, LATENT), BF), sds((2, HALF, 128), BF), sds((HALF, 128), F32)),
        0, len(pieces), flops=1_500_000_000, nbytes=1 << 20)(*pieces)
    kc, vs, *weights = call(
        keys_kernel,
        (sds((4, HALF, 256), BF), sds((4, HALF, 128), BF), *([sds((512, 512), BF)] * (2 if hand_on else 0))),
        0, 4, flops=500_000_000, nbytes=2 << 20)(latents, ropes, wk, wv)
    return kc, vs, latents, marks, *weights


def stats_kernel(where, q0, q1, q2, q3, kc0, kc1, vs0, vs1, marks0, marks1, qc, gs, es, dps, stats, bias, qid):
    xi, zi = where[0], where[1]
    for s, block in enumerate((q0, q1, q2, q3)):
        at = pl.ds(pl.multiple_of(((xi + s) & 3) * 128, 128), 128)

        def rows(first, count=128):
            return block[first:first + count, :]

        for h in range(HEADS):
            qc[h, at, 0:128] = rows(h * 128)
            qc[h, at, 128:256] = rows(1024 + h // 2 * 128)
            gs[h, at, :] = rows(512 + h * 128)
        qid[:, at] = rows(1280, 16)
    q_marks = qid[0:1, :].astype(F32)
    q_pos = zi * QROWS + lax.broadcasted_iota(jnp.int32, (128, QROWS), 1)
    for j in range(REACH):
        at = slice(j * 128, j * 128 + 128)
        first = ((zi - ORDER[j]) & (Z - 1)) * QROWS + xi * 128
        k_pos = first + lax.broadcasted_iota(jnp.int32, (128, QROWS), 0)
        allowed = (k_pos <= q_pos) & ((marks0, marks1)[j // 2][j % 2 * 128:j % 2 * 128 + 128, 64:65] == q_marks)
        bias[at, :] = jnp.where(allowed, 0.0, NEG)
    for h in range(HEADS):
        for b in range(0, QROWS, 256):
            sl = slice(b, b + 256)
            parts = []
            for n, (kc, vs) in enumerate(((kc0, vs0), (kc1, vs1))):
                at = slice(n * HALF, (n + 1) * HALF)
                s = lax.dot_general(kc[h], qc[h, sl, :], NT, preferred_element_type=F32) * SCALE + bias[at, sl]
                dp = lax.dot_general(vs[h], gs[h, sl, :], NT, preferred_element_type=F32)
                dps[h, at, sl] = dp
                parts.append((at, s, dp))
            m = jnp.maximum(*[jnp.max(s, axis=0, keepdims=True) for _, s, _ in parts])
            total = cross = 0.0
            for at, s, dp in parts:
                e = jnp.exp(s - m)
                es[h, at, sl] = e
                total = total + jnp.sum(e, axis=0, keepdims=True)
                cross = cross + jnp.sum(e * dp, axis=0, keepdims=True)
            stats[h:h + 1, sl] = m
            stats[4 + h:5 + h, sl] = total
            stats[8 + h:9 + h, sl] = cross
    stats[12:16, :] = jnp.zeros((4, QROWS), F32)


def run_stats(where, qs, *keys):
    sds = jax.ShapeDtypeStruct
    return call(
        stats_kernel,
        (sds((4, QROWS, 256), BF), sds((4, QROWS, 128), BF),
         sds((4, KROWS, QROWS), F32), sds((4, KROWS, QROWS), F32), sds((16, QROWS), F32)),
        1, 10, scratch=[pltpu.VMEM((KROWS, QROWS), F32), pltpu.VMEM((16, QROWS), BF)],
        flops=1_000_000_000, nbytes=8 << 20,
    )(where, *qs, *keys)


def weight_kernel(where, t0, t1, t2, t3, qc, gs, es, dps, latents0, latents1, wk, wv, w_keep, w_far, w_send, ds, dkv, tail, d3,
                  p_scr, w_scr):
    xi, core = where[0], where[2]
    tops = [t[0:4, :] for t in (t0, t1, t2, t3)]
    top = functools.reduce(jnp.maximum, tops)
    total = jnp.zeros((4, QROWS), F32)
    cross = jnp.zeros((4, QROWS), F32)
    for t, m in zip((t0, t1, t2, t3), tops):
        f = jnp.exp(m - top)
        total = total + f * t[4:8, :]
        cross = cross + f * t[8:12, :]
    inv = 1.0 / total
    delta = cross * inv
    scaled = jnp.exp(tops[0] - top) * inv
    rope_grad = [jnp.zeros((KROWS, 128), F32), jnp.zeros((KROWS, 128), F32)]
    for h in range(HEADS):
        for b in range(0, QROWS, 256):
            sl = slice(b, b + 256)
            p = es[h, :, sl] * scaled[h:h + 1, sl]
            p_scr[h % 2, :, sl] = p.astype(BF)
            ds[h, :, sl] = (p * (dps[h, :, sl] - delta[h:h + 1, sl]) * SCALE).astype(BF)
        cols = slice(h * 128, (h + 1) * 128)
        dkv[1, :, cols] = jnp.dot(p_scr[h % 2], gs[h], preferred_element_type=F32).astype(BF)
        dk = jnp.dot(ds[h], qc[h], preferred_element_type=F32)
        dkv[0, :, cols] = dk[:, :128].astype(BF)
        rope_grad[h % 2] = rope_grad[h % 2] + dk[:, 128:]
    for out, which in ((w_scr, 1 - core), (w_keep, core)):
        w = (lax.dot_general(dkv[which, :HALF], latents0[...], TN, preferred_element_type=F32)
             + lax.dot_general(dkv[which, HALF:], latents1[...], TN, preferred_element_type=F32)).astype(BF)
        for r in range(32):
            out[(r - xi) & 3, r // 4 * 16:r // 4 * 16 + 16, :] = w[r * 16:r * 16 + 16, :]
    w_far[...] = w_scr[2]
    for n, s in enumerate((0, 1, 3)):
        w_send[n] = w_scr[s]
    lane = lax.broadcasted_iota(jnp.int32, (KROWS, 128), 1)
    tail[...] = jnp.where(lane < 64, rope_grad[0] + pltpu.roll(rope_grad[1], 64, 1), 0.0).astype(BF)
    far = slice(3 * ROWS, KROWS)
    d3[:, :512] = (lax.dot_general(dkv[0, far], wk[...], NT, preferred_element_type=F32)
                   + lax.dot_general(dkv[1, far], wv[...], NT, preferred_element_type=F32)).astype(BF)
    d3[:, 512:640] = tail[far, :]


def run_weight(where, ts, *mats):
    sds = jax.ShapeDtypeStruct
    return call(
        weight_kernel,
        (sds((4, 128, 512), BF), sds((128, 512), BF), sds((3, 128, 512), BF), sds((4, KROWS, QROWS), BF), sds((2, KROWS, 512), BF),
         sds((KROWS, 128), BF), sds((128, 640), BF)),
        1, 12, scratch=[pltpu.VMEM((2, KROWS, QROWS), BF), pltpu.VMEM((4, 128, 512), BF)], flops=1_500_000_000, nbytes=10 << 20,
    )(where, *ts, *mats)


def grads_kernel(where, ds, dkv, tail, kc0, kc1, wk, wv, d0, d1, d2, o0, o1, o2, o3, dq):
    xi = where[0]
    near = slice(0, 3 * ROWS)
    lat = (lax.dot_general(dkv[0, near], wk[...], NT, preferred_element_type=F32)
           + lax.dot_general(dkv[1, near], wv[...], NT, preferred_element_type=F32)).astype(BF)
    for j, d in enumerate((d1, d2, d0)):
        d[:, :512] = lat[j * 128:(j + 1) * 128, :]
        d[:, 512:640] = tail[j * 128:(j + 1) * 128, :]
    for p in range(2):
        pair = 0.0
        for h in (2 * p, 2 * p + 1):
            dqh = (lax.dot_general(ds[h, :HALF], kc0[h], TN, preferred_element_type=F32)
                   + lax.dot_general(ds[h, HALF:], kc1[h], TN, preferred_element_type=F32))
            dq[:, h * 128:(h + 1) * 128] = dqh[:, :128].astype(BF)
            pair = pair + dqh[:, 128:]
        dq[:, 512 + p * 128:640 + p * 128] = pair.astype(BF)
    for s, o in enumerate((o0, o1, o2, o3)):
        o[...] = dq[pl.ds(pl.multiple_of(((xi + s) & 3) * 128, 128), 128), :]


def run_grads(where, ds, dkv, tail, kc0, kc1, wk, wv):
    sds = jax.ShapeDtypeStruct
    return call(
        grads_kernel,
        tuple([sds((128, 640), BF)] * 3 + [sds((128, 768), BF)] * 4),
        1, 7, scratch=[pltpu.VMEM((QROWS, 768), BF)], flops=1_500_000_000, nbytes=10 << 20,
    )(where, ds, dkv, tail, kc0, kc1, wk, wv)


def far_sum_kernel(keep, far, out):
    out[...] = (keep[2].astype(F32) + far[...].astype(F32)).astype(BF)


def near_sum_kernel(keep, near, out1, out3):
    out1[...] = (keep[1].astype(F32) + near[1].astype(F32)).astype(BF)
    out3[...] = (keep[3].astype(F32) + near[2].astype(F32)).astype(BF)


def sum_x_kernel(keep, near, p1, p2, p3, out):
    out[...] = (keep[0].astype(F32) + near[0].astype(F32) + wide(p1, p2, p3)).astype(BF)


def wide(*refs):
    return functools.reduce(jnp.add, [r[...].astype(F32) for r in refs])


def sum_kernel(*refs):
    refs[-1][...] = wide(*refs[:-1]).astype(refs[-1].dtype)


def add_up(*parts, dtype=BF):
    return call(sum_kernel, jax.ShapeDtypeStruct(parts[0].shape, dtype), 0, len(parts), nbytes=1 << 20)(*parts)


def sum_z_kernel(parts, w):
    w[...] = jnp.sum(parts[...].reshape(Z, 16, 512).astype(F32), axis=0).astype(BF)


def query_kernel(q0, q1, q2, q3, nope, rope):
    q = wide(q0, q1, q2, q3).astype(BF)
    nope[...] = q[:, :512]
    rope[...] = q[:, 512:]


def latent_kernel(part, d1, latent):
    latent[...] = wide(part, d1).astype(BF)[:, :576].T


def body(kv_latent, q_nope, q_rope, w_key_up, w_value_up, out_grad, segment_ids):
    ctx = lax.axis_index("ctx")
    dp = lax.axis_index("dp")
    core = dp % 2
    where = jnp.stack([ctx % X, ctx // X, core]).astype(jnp.int32)
    q, *c = pack(q_nope[0], q_rope[0], out_grad[0], kv_latent[0].T, segment_ids)
    c1 = [z_shift(v, 1) for v in c]
    c2 = [z_shift(v, 1) for v in c1]
    kc0, vs0, latents0, marks0, wk, wv = run_keys(c1 + c2, w_key_up, w_value_up, True)
    c3 = [z_shift(v, 1) for v in c2]
    later, _ = lax.optimization_barrier((q, c1))
    qs = (q, x_shift(q, -1), x_shift(q, 2), x_shift(later, 1))
    kc1, vs1, latents1, marks1 = run_keys(c + c3, wk, wv, False)
    qc, gs, es, dps, stats = run_stats(where, qs, kc0, kc1, vs0, vs1, marks0, marks1)
    ts = (stats, x_shift(stats, 1), x_shift(stats, 2), x_shift(stats, -1))
    w_keep, w_far, w_send, ds, dkv, tail, d3 = run_weight(where, ts, qc, gs, es, dps, latents0, latents1, wk, wv)
    w_far, near = core_swap(w_far), core_swap(w_send)
    d0, d1, d2, o0, o1, o2, o3 = run_grads(where, ds, dkv, tail, kc0, kc1, wk, wv)
    sds = jax.ShapeDtypeStruct
    piece = sds((128, 512), BF)
    p2 = call(far_sum_kernel, piece, 0, 2, nbytes=1 << 18)(w_keep, w_far)
    p1, p3 = call(near_sum_kernel, (piece, piece), 0, 2, nbytes=1 << 19)(w_keep, near)
    w = call(sum_x_kernel, piece, 0, 5, nbytes=1 << 20)(w_keep, near, x_shift(p1, 1), x_shift(p2, 2), x_shift(p3, -1))
    w = lax.all_to_all(w, "ctx", 0, 0, tiled=True, axis_index_groups=[[z * X + x for z in range(Z)] for x in range(X)])
    d = add_up(z_shift(d3, -1), d2)
    d = call(sum_kernel, sds((128, 640), F32), 0, 2, flops=1_000_000_000, nbytes=1 << 20)(z_shift(d, -2), d0)
    w, d = lax.optimization_barrier((w, d))
    w = call(sum_z_kernel, sds((16, 512), BF), 0, 1, nbytes=1 << 18)(w)
    w = add_up(w, y_pair(w, False))
    other = y_pair(w, True)
    grad_nope, grad_rope = call(query_kernel, (sds((128, 512), BF), sds((128, 256), BF)), 0, 4, nbytes=1 << 20)(
        o0, x_shift(o1, 1), x_shift(o2, 2), x_shift(o3, -1))
    grad_latent = call(latent_kernel, sds((576, 128), BF), 0, 2, nbytes=1 << 20)(d, z_shift(d1, -1))
    w, grad_nope, grad_latent = lax.optimization_barrier((w, grad_nope, grad_latent))
    w = add_up(w, other, dtype=F32)
    other = core_swap(w)
    grad_key = jnp.where(core == 0, w, other)
    grad_value = jnp.where(core == 0, other, w)
    return grad_nope[None], grad_rope[None], grad_latent.T[None], grad_key, grad_value


def solution(mesh):
    return jax.shard_map(
        body,
        mesh=mesh,
        in_specs=(
            P("dp", "ctx", None),
            P("dp", "ctx", None),
            P("dp", "ctx", None),
            P(),
            P(),
            P("dp", "ctx", None),
            P("dp", "ctx"),
        ),
        out_specs=(
            P("dp", "ctx", None),
            P("dp", "ctx", None),
            P("dp", "ctx", None),
            P("ctx", None),
            P("ctx", None),
        ),
        check_vma=False,
    )
```

```python
import functools

import jax
import jax.numpy as jnp
from jax import lax
from jax.experimental import pallas as pl
from jax.experimental.pallas import tpu as pltpu
from jax.sharding import PartitionSpec as P

Z, X, Y = 8, 4, 4
HEADS, HEAD, ROPE, LATENT = 4, 128, 64, 512
ROWS = 128
REACH = 4
QROWS = X * ROWS
KROWS = REACH * ROWS
HALF = KROWS // 2
ORDER = (1, 2, 0, 3)
SCALE = (HEAD + ROPE) ** -0.5
NEG = -1e30
CUTS = (64, 64)
PACK_VMEM = 60.5
BF, F32 = jnp.bfloat16, jnp.float32
NT = (((1,), (1,)), ((), ()))
TN = (((0,), (0,)), ((), ()))
VMEM = pl.BlockSpec(memory_space=pltpu.VMEM)
SMEM = pl.BlockSpec(memory_space=pltpu.SMEM)
HBM = pl.BlockSpec(memory_space=pltpu.HBM)


def x_shift(v, s):
    return lax.ppermute(v, "ctx", [(i, i // X * X + (i % X + s) % X) for i in range(Z * X)])


def z_shift(v, s):
    return lax.ppermute(v, "ctx", [(i, (i + s * X) % (Z * X)) for i in range(Z * X)])


def y_pair(v, far):
    pairs = [(i, 2 * ((Y - 1 - i // 2) if far else (i // 2 ^ 1)) + i % 2) for i in range(2 * Y)]
    return lax.ppermute(v, "dp", pairs)


def core_swap(v):
    return lax.ppermute(v, "dp", [(i, i ^ 1) for i in range(2 * Y)])


def call(kernel, out_shape, n_smem, n_vmem, n_hbm=0, scratch=(), flops=0, nbytes=0, vmem=16):
    return pl.pallas_call(
        kernel,
        out_shape=out_shape,
        in_specs=[SMEM] * n_smem + [VMEM] * n_vmem + [HBM] * n_hbm,
        out_specs=jax.tree.map(lambda _: VMEM, out_shape),
        scratch_shapes=list(scratch),
        compiler_params=pltpu.CompilerParams(vmem_limit_bytes=int(vmem * (1 << 20))),
        cost_estimate=pl.CostEstimate(flops=flops, bytes_accessed=nbytes, transcendentals=0),
    )


def pack_kernel(nope, rope, grad, kv_t, ids, q_out, *rest):
    *c_outs, kv_scr, ids_scr, sems = rest
    copies = [pltpu.make_async_copy(kv_t, kv_scr, sems.at[0]), pltpu.make_async_copy(ids, ids_scr, sems.at[1])]
    for n, (source, parts) in enumerate(((nope, 4), (grad, 4), (rope, 2))):
        for i in range(parts):
            at = n * 512 + i * 128
            copies.append(pltpu.make_async_copy(
                source.at[:, i * 128:(i + 1) * 128], q_out.at[at:at + 128, :], sems.at[len(copies)]))
    for copy in copies:
        copy.start()
    copies[0].wait()
    copies[1].wait()
    marks = jnp.broadcast_to(ids_scr[...].astype(F32), (128, 128)).astype(BF)
    q_out[1280:1296, :] = marks[:16]
    rows = jnp.concatenate([kv_scr[...], marks[:64]], axis=0).T
    first = 0
    for c_out in c_outs:
        c_out[...] = rows[first:first + c_out.shape[0]]
        first += c_out.shape[0]
    for copy in copies[2:]:
        copy.wait()


def pack(nope, rope, grad, kv_t, ids):
    pieces = [jax.ShapeDtypeStruct((rows, 640), BF) for rows in CUTS]
    return call(
        pack_kernel, (jax.ShapeDtypeStruct((1296, 128), BF), *pieces), 0, 0, 5,
        scratch=[pltpu.VMEM((576, 128), BF), pltpu.VMEM((1, 128), jnp.int32), pltpu.SemaphoreType.DMA((12,))],
        nbytes=1 << 20, vmem=PACK_VMEM)(nope, rope, grad, kv_t, ids)


def open_kernel(*refs):
    pieces, (latents, ropes, marks) = refs[:-3], refs[-3:]
    first = 0
    for c in pieces:
        at = slice(first, first + c.shape[0])
        first += c.shape[0]
        latents[at, :] = c[:, :512]
        tail = c[:, 512:640].astype(F32)
        marks[at, :] = tail
        even = jnp.where(lax.broadcasted_iota(jnp.int32, tail.shape, 1) < 64, tail, 0.0)
        ropes[0, at, :] = even.astype(BF)
        ropes[1, at, :] = pltpu.roll(even, 64, 1).astype(BF)


def keys_kernel(latents, ropes, wk, wv, kc, vs, *weights):
    keys = jnp.dot(latents[...], wk[...], preferred_element_type=F32).astype(BF)
    values = jnp.dot(latents[...], wv[...], preferred_element_type=F32).astype(BF)
    for h in range(HEADS):
        kc[h, :, 0:128] = keys[:, h * 128:(h + 1) * 128]
        kc[h, :, 128:256] = ropes[h % 2]
        vs[h, :, :] = values[:, h * 128:(h + 1) * 128]
    for out, w in zip(weights, (wk, wv)):
        out[...] = w[...]


def run_keys(pieces, wk, wv, hand_on):
    sds = jax.ShapeDtypeStruct
    latents, ropes, marks = call(
        open_kernel, (sds((HALF, LATENT), BF), sds((2, HALF, 128), BF), sds((HALF, 128), F32)),
        0, len(pieces), flops=1_500_000_000, nbytes=1 << 20)(*pieces)
    kc, vs, *weights = call(
        keys_kernel,
        (sds((4, HALF, 256), BF), sds((4, HALF, 128), BF), *([sds((512, 512), BF)] * (2 if hand_on else 0))),
        0, 4, flops=500_000_000, nbytes=2 << 20)(latents, ropes, wk, wv)
    return kc, vs, latents, marks, *weights


def columns(blocks, first):
    return jnp.concatenate([q[first:first + 128, :] for q in blocks], axis=0)


def queries_of(blocks, h):
    return jnp.concatenate([columns(blocks, h * 128), columns(blocks, 1024 + h // 2 * 128)], axis=1)


def stats_kernel(where, q0, q1, q2, q3, kc0, kc1, vs0, vs1, marks0, marks1, es, dps, stats, bias):
    xi, zi = where[0], where[1]
    blocks = (q0, q1, q2, q3)
    q_marks = jnp.concatenate([q[1280:1296, :] for q in blocks], axis=1)[0:1].astype(F32)
    lane = lax.broadcasted_iota(jnp.int32, (128, QROWS), 1)
    q_pos = zi * QROWS + ((xi + (lane >> 7)) & 3) * 128 + (lane & 127)
    for j in range(REACH):
        at = slice(j * 128, j * 128 + 128)
        first = ((zi - ORDER[j]) & (Z - 1)) * QROWS + xi * 128
        k_pos = first + lax.broadcasted_iota(jnp.int32, (128, QROWS), 0)
        allowed = (k_pos <= q_pos) & ((marks0, marks1)[j // 2][j % 2 * 128:j % 2 * 128 + 128, 64:65] == q_marks)
        bias[at, :] = jnp.where(allowed, 0.0, NEG)
    for h in range(HEADS):
        for b in range(0, QROWS, 256):
            sl = slice(b, b + 256)
            pair = blocks[b // 128:b // 128 + 2]
            qc, gs = queries_of(pair, h), columns(pair, 512 + h * 128)
            parts = []
            for n, (kc, vs) in enumerate(((kc0, vs0), (kc1, vs1))):
                at = slice(n * HALF, (n + 1) * HALF)
                s = lax.dot_general(kc[h], qc, NT, preferred_element_type=F32) * SCALE + bias[at, sl]
                dp = lax.dot_general(vs[h], gs, NT, preferred_element_type=F32)
                dps[h, at, sl] = dp
                parts.append((at, s, dp))
            m = jnp.maximum(*[jnp.max(s, axis=0, keepdims=True) for _, s, _ in parts])
            total = cross = 0.0
            for at, s, dp in parts:
                e = jnp.exp(s - m)
                es[h, at, sl] = e
                total = total + jnp.sum(e, axis=0, keepdims=True)
                cross = cross + jnp.sum(e * dp, axis=0, keepdims=True)
            stats[h:h + 1, sl] = m
            stats[4 + h:5 + h, sl] = total
            stats[8 + h:9 + h, sl] = cross
    stats[12:16, :] = jnp.zeros((4, QROWS), F32)


def run_stats(where, *mats):
    sds = jax.ShapeDtypeStruct
    return call(
        stats_kernel, (sds((4, KROWS, QROWS), F32), sds((4, KROWS, QROWS), F32), sds((16, QROWS), F32)),
        1, 10, scratch=[pltpu.VMEM((KROWS, QROWS), F32)], flops=1_000_000_000, nbytes=8 << 20,
    )(where, *mats)


def weight_kernel(where, t0, t1, t2, t3, q0, q1, q2, q3, es, dps, latents0, latents1, wk, wv, w_keep, w_far, w_send, ds, dkv, tail, d3,
                  p_scr, w_scr):
    xi, core = where[0], where[2]
    blocks = (q0, q1, q2, q3)
    ts = [t[...] if s == 0 else jnp.concatenate([t[:, 512 - s * 128:], t[:, :512 - s * 128]], axis=1)
          for s, t in enumerate((t0, t1, t2, t3))]
    tops = [t[0:4] for t in ts]
    top = functools.reduce(jnp.maximum, tops)
    total = jnp.zeros((4, QROWS), F32)
    cross = jnp.zeros((4, QROWS), F32)
    for t, m in zip(ts, tops):
        f = jnp.exp(m - top)
        total = total + f * t[4:8]
        cross = cross + f * t[8:12]
    inv = 1.0 / total
    delta = cross * inv
    scaled = jnp.exp(tops[0] - top) * inv
    rope_grad = [jnp.zeros((KROWS, 128), F32), jnp.zeros((KROWS, 128), F32)]
    for h in range(HEADS):
        for b in range(0, QROWS, 256):
            sl = slice(b, b + 256)
            p = es[h, :, sl] * scaled[h:h + 1, sl]
            p_scr[h % 2, :, sl] = p.astype(BF)
            ds[h, :, sl] = (p * (dps[h, :, sl] - delta[h:h + 1, sl]) * SCALE).astype(BF)
        cols = slice(h * 128, (h + 1) * 128)
        dkv[1, :, cols] = jnp.dot(p_scr[h % 2], columns(blocks, 512 + h * 128), preferred_element_type=F32).astype(BF)
        dk = jnp.dot(ds[h], queries_of(blocks, h), preferred_element_type=F32)
        dkv[0, :, cols] = dk[:, :128].astype(BF)
        rope_grad[h % 2] = rope_grad[h % 2] + dk[:, 128:]
    for out, which in ((w_scr, 1 - core), (w_keep, core)):
        w = (lax.dot_general(dkv[which, :HALF], latents0[...], TN, preferred_element_type=F32)
             + lax.dot_general(dkv[which, HALF:], latents1[...], TN, preferred_element_type=F32)).astype(BF)
        for r in range(32):
            out[(r - xi) & 3, r // 4 * 16:r // 4 * 16 + 16, :] = w[r * 16:r * 16 + 16, :]
    w_far[...] = w_scr[2]
    for n, s in enumerate((0, 1, 3)):
        w_send[n] = w_scr[s]
    lane = lax.broadcasted_iota(jnp.int32, (KROWS, 128), 1)
    tail[...] = jnp.where(lane < 64, rope_grad[0] + pltpu.roll(rope_grad[1], 64, 1), 0.0).astype(BF)
    far = slice(3 * ROWS, KROWS)
    d3[:, :512] = (lax.dot_general(dkv[0, far], wk[...], NT, preferred_element_type=F32)
                   + lax.dot_general(dkv[1, far], wv[...], NT, preferred_element_type=F32)).astype(BF)
    d3[:, 512:640] = tail[far, :]


def run_weight(where, ts, *mats):
    sds = jax.ShapeDtypeStruct
    return call(
        weight_kernel,
        (sds((4, 128, 512), BF), sds((128, 512), BF), sds((3, 128, 512), BF), sds((4, KROWS, QROWS), BF), sds((2, KROWS, 512), BF),
         sds((KROWS, 128), BF), sds((128, 640), BF)),
        1, 14, scratch=[pltpu.VMEM((2, KROWS, QROWS), BF), pltpu.VMEM((4, 128, 512), BF)], flops=1_500_000_000, nbytes=10 << 20,
    )(where, *ts, *mats)


def grads_kernel(where, ds, dkv, tail, kc0, kc1, wk, wv, d0, d1, d2, o0, o1, o2, o3, dq):
    near = slice(0, 3 * ROWS)
    lat = (lax.dot_general(dkv[0, near], wk[...], NT, preferred_element_type=F32)
           + lax.dot_general(dkv[1, near], wv[...], NT, preferred_element_type=F32)).astype(BF)
    for j, d in enumerate((d1, d2, d0)):
        d[:, :512] = lat[j * 128:(j + 1) * 128, :]
        d[:, 512:640] = tail[j * 128:(j + 1) * 128, :]
    for p in range(2):
        pair = 0.0
        for h in (2 * p, 2 * p + 1):
            dqh = (lax.dot_general(ds[h, :HALF], kc0[h], TN, preferred_element_type=F32)
                   + lax.dot_general(ds[h, HALF:], kc1[h], TN, preferred_element_type=F32))
            dq[:, h * 128:(h + 1) * 128] = dqh[:, :128].astype(BF)
            pair = pair + dqh[:, 128:]
        dq[:, 512 + p * 128:640 + p * 128] = pair.astype(BF)
    for s, o in enumerate((o0, o1, o2, o3)):
        o[...] = dq[s * 128:(s + 1) * 128, :]


def run_grads(where, ds, dkv, tail, kc0, kc1, wk, wv):
    sds = jax.ShapeDtypeStruct
    return call(
        grads_kernel,
        tuple([sds((128, 640), BF)] * 3 + [sds((128, 768), BF)] * 4),
        1, 7, scratch=[pltpu.VMEM((QROWS, 768), BF)], flops=1_500_000_000, nbytes=10 << 20,
    )(where, ds, dkv, tail, kc0, kc1, wk, wv)


def far_sum_kernel(keep, far, out):
    out[...] = (keep[2].astype(F32) + far[...].astype(F32)).astype(BF)


def near_sum_kernel(keep, near, out1, out3):
    out1[...] = (keep[1].astype(F32) + near[1].astype(F32)).astype(BF)
    out3[...] = (keep[3].astype(F32) + near[2].astype(F32)).astype(BF)


def sum_x_kernel(keep, near, p1, p2, p3, out):
    out[...] = (keep[0].astype(F32) + near[0].astype(F32) + wide(p1, p2, p3)).astype(BF)


def wide(*refs):
    return functools.reduce(jnp.add, [r[...].astype(F32) for r in refs])


def sum_kernel(*refs):
    refs[-1][...] = wide(*refs[:-1]).astype(refs[-1].dtype)


def add_up(*parts, dtype=BF):
    return call(sum_kernel, jax.ShapeDtypeStruct(parts[0].shape, dtype), 0, len(parts), nbytes=1 << 20)(*parts)


def sum_z_kernel(parts, w):
    w[...] = jnp.sum(parts[...].reshape(Z, 16, 512).astype(F32), axis=0).astype(BF)


def query_kernel(q0, q1, q2, q3, nope, rope):
    q = wide(q0, q1, q2, q3).astype(BF)
    nope[...] = q[:, :512]
    rope[...] = q[:, 512:]


def latent_kernel(part, d1, latent):
    latent[...] = wide(part, d1).astype(BF)[:, :576].T


def body(kv_latent, q_nope, q_rope, w_key_up, w_value_up, out_grad, segment_ids):
    ctx = lax.axis_index("ctx")
    dp = lax.axis_index("dp")
    core = dp % 2
    where = jnp.stack([ctx % X, ctx // X, core]).astype(jnp.int32)
    q, *c = pack(q_nope[0], q_rope[0], out_grad[0], kv_latent[0].T, segment_ids)
    c1 = [z_shift(v, 1) for v in c]
    c2 = [z_shift(v, 1) for v in c1]
    kc0, vs0, latents0, marks0, wk, wv = run_keys(c1 + c2, w_key_up, w_value_up, True)
    c3 = [z_shift(v, 1) for v in c2]
    later, _ = lax.optimization_barrier((q, c1))
    qs = (q, x_shift(q, -1), x_shift(q, 2), x_shift(later, 1))
    kc1, vs1, latents1, marks1 = run_keys(c + c3, wk, wv, False)
    es, dps, stats = run_stats(where, *qs, kc0, kc1, vs0, vs1, marks0, marks1)
    ts = (stats, x_shift(stats, -1), x_shift(stats, 2), x_shift(stats, 1))
    w_keep, w_far, w_send, ds, dkv, tail, d3 = run_weight(where, ts, *qs, es, dps, latents0, latents1, wk, wv)
    w_far, near = core_swap(w_far), core_swap(w_send)
    d0, d1, d2, o0, o1, o2, o3 = run_grads(where, ds, dkv, tail, kc0, kc1, wk, wv)
    sds = jax.ShapeDtypeStruct
    piece = sds((128, 512), BF)
    p2 = call(far_sum_kernel, piece, 0, 2, nbytes=1 << 18)(w_keep, w_far)
    p1, p3 = call(near_sum_kernel, (piece, piece), 0, 2, nbytes=1 << 19)(w_keep, near)
    w = call(sum_x_kernel, piece, 0, 5, nbytes=1 << 20)(w_keep, near, x_shift(p1, 1), x_shift(p2, 2), x_shift(p3, -1))
    w = lax.all_to_all(w, "ctx", 0, 0, tiled=True, axis_index_groups=[[z * X + x for z in range(Z)] for x in range(X)])
    d = add_up(z_shift(d3, -1), d2)
    d = call(sum_kernel, sds((128, 640), F32), 0, 2, flops=1_000_000_000, nbytes=1 << 20)(z_shift(d, -2), d0)
    w, d = lax.optimization_barrier((w, d))
    w = call(sum_z_kernel, sds((16, 512), BF), 0, 1, nbytes=1 << 18)(w)
    w = add_up(w, y_pair(w, False))
    other = y_pair(w, True)
    grad_nope, grad_rope = call(query_kernel, (sds((128, 512), BF), sds((128, 256), BF)), 0, 4, flops=1_000_000_000, nbytes=1 << 20)(
        o0, x_shift(o1, 1), x_shift(o2, 2), x_shift(o3, -1))
    grad_latent = call(latent_kernel, sds((576, 128), BF), 0, 2, nbytes=1 << 20)(d, z_shift(d1, -1))
    w, grad_latent = lax.optimization_barrier((w, grad_latent))
    w = add_up(w, other, dtype=F32)
    other = core_swap(w)
    grad_key = jnp.where(core == 0, w, other)
    grad_value = jnp.where(core == 0, other, w)
    return grad_nope[None], grad_rope[None], grad_latent.T[None], grad_key, grad_value


def solution(mesh):
    return jax.shard_map(
        body,
        mesh=mesh,
        in_specs=(
            P("dp", "ctx", None),
            P("dp", "ctx", None),
            P("dp", "ctx", None),
            P(),
            P(),
            P("dp", "ctx", None),
            P("dp", "ctx"),
        ),
        out_specs=(
            P("dp", "ctx", None),
            P("dp", "ctx", None),
            P("dp", "ctx", None),
            P("ctx", None),
            P("ctx", None),
        ),
        check_vma=False,
    )
```

```python
import functools

import jax
import jax.numpy as jnp
from jax import lax
from jax.experimental import pallas as pl
from jax.experimental.pallas import tpu as pltpu
from jax.sharding import PartitionSpec as P

Z, X, Y = 8, 4, 4
HEADS, HEAD, ROPE, LATENT = 4, 128, 64, 512
ROWS = 128
REACH = 4
QROWS = X * ROWS
KROWS = REACH * ROWS
HALF = KROWS // 2
ORDER = (1, 2, 0, 3)
SCALE = (HEAD + ROPE) ** -0.5
NEG = -1e30
CUTS = (64, 64)
PACK_VMEM = 60.5
BF, F32 = jnp.bfloat16, jnp.float32
NT = (((1,), (1,)), ((), ()))
TN = (((0,), (0,)), ((), ()))
VMEM = pl.BlockSpec(memory_space=pltpu.VMEM)
SMEM = pl.BlockSpec(memory_space=pltpu.SMEM)
HBM = pl.BlockSpec(memory_space=pltpu.HBM)


def x_shift(v, s):
    return lax.ppermute(v, "ctx", [(i, i // X * X + (i % X + s) % X) for i in range(Z * X)])


def z_shift(v, s):
    return lax.ppermute(v, "ctx", [(i, (i + s * X) % (Z * X)) for i in range(Z * X)])


def y_pair(v, far):
    pairs = [(i, 2 * ((Y - 1 - i // 2) if far else (i // 2 ^ 1)) + i % 2) for i in range(2 * Y)]
    return lax.ppermute(v, "dp", pairs)


def core_swap(v):
    return lax.ppermute(v, "dp", [(i, i ^ 1) for i in range(2 * Y)])


def call(kernel, out_shape, n_smem, n_vmem, n_hbm=0, scratch=(), flops=0, nbytes=0, vmem=16):
    return pl.pallas_call(
        kernel,
        out_shape=out_shape,
        in_specs=[SMEM] * n_smem + [VMEM] * n_vmem + [HBM] * n_hbm,
        out_specs=jax.tree.map(lambda _: VMEM, out_shape),
        scratch_shapes=list(scratch),
        compiler_params=pltpu.CompilerParams(vmem_limit_bytes=int(vmem * (1 << 20))),
        cost_estimate=pl.CostEstimate(flops=flops, bytes_accessed=nbytes, transcendentals=0),
    )


def pack_kernel(nope, rope, grad, kv_t, ids, q_out, *rest):
    *c_outs, kv_scr, ids_scr, sems = rest
    copies = [pltpu.make_async_copy(kv_t, kv_scr, sems.at[0]), pltpu.make_async_copy(ids, ids_scr, sems.at[1])]
    for n, (source, parts) in enumerate(((nope, 4), (grad, 4), (rope, 2))):
        for i in range(parts):
            at = n * 512 + i * 128
            copies.append(pltpu.make_async_copy(
                source.at[:, i * 128:(i + 1) * 128], q_out.at[at:at + 128, :], sems.at[len(copies)]))
    for copy in copies:
        copy.start()
    copies[0].wait()
    copies[1].wait()
    marks = jnp.broadcast_to(ids_scr[...].astype(F32), (128, 128)).astype(BF)
    q_out[1280:1296, :] = marks[:16]
    rows = jnp.concatenate([kv_scr[...], marks[:64]], axis=0).T
    first = 0
    for c_out in c_outs:
        c_out[...] = rows[first:first + c_out.shape[0]]
        first += c_out.shape[0]
    for copy in copies[2:]:
        copy.wait()


def pack(nope, rope, grad, kv_t, ids):
    pieces = [jax.ShapeDtypeStruct((rows, 640), BF) for rows in CUTS]
    return call(
        pack_kernel, (jax.ShapeDtypeStruct((1296, 128), BF), *pieces), 0, 0, 5,
        scratch=[pltpu.VMEM((576, 128), BF), pltpu.VMEM((1, 128), jnp.int32), pltpu.SemaphoreType.DMA((12,))],
        nbytes=1 << 20, vmem=PACK_VMEM)(nope, rope, grad, kv_t, ids)


def open_kernel(*refs):
    pieces, (latents, ropes, marks) = refs[:-3], refs[-3:]
    first = 0
    for c in pieces:
        at = slice(first, first + c.shape[0])
        first += c.shape[0]
        latents[at, :] = c[:, :512]
        tail = c[:, 512:640].astype(F32)
        marks[at, :] = tail
        even = jnp.where(lax.broadcasted_iota(jnp.int32, tail.shape, 1) < 64, tail, 0.0)
        ropes[0, at, :] = even.astype(BF)
        ropes[1, at, :] = pltpu.roll(even, 64, 1).astype(BF)


def keys_kernel(latents, ropes, wk, wv, kc, vs, *weights):
    keys = jnp.dot(latents[...], wk[...], preferred_element_type=F32).astype(BF)
    values = jnp.dot(latents[...], wv[...], preferred_element_type=F32).astype(BF)
    for h in range(HEADS):
        kc[h, :, 0:128] = keys[:, h * 128:(h + 1) * 128]
        kc[h, :, 128:256] = ropes[h % 2]
        vs[h, :, :] = values[:, h * 128:(h + 1) * 128]
    for out, w in zip(weights, (wk, wv)):
        out[...] = w[...]


def run_keys(pieces, wk, wv, hand_on):
    sds = jax.ShapeDtypeStruct
    latents, ropes, marks = call(
        open_kernel, (sds((HALF, LATENT), BF), sds((2, HALF, 128), BF), sds((HALF, 128), F32)),
        0, len(pieces), flops=1_500_000_000, nbytes=1 << 20)(*pieces)
    kc, vs, *weights = call(
        keys_kernel,
        (sds((4, HALF, 256), BF), sds((4, HALF, 128), BF), *([sds((512, 512), BF)] * (2 if hand_on else 0))),
        0, 4, flops=500_000_000, nbytes=2 << 20)(latents, ropes, wk, wv)
    return kc, vs, latents, marks, *weights


def columns(blocks, first):
    return jnp.concatenate([q[first:first + 128, :] for q in blocks], axis=0)


def queries_of(blocks, h):
    return jnp.concatenate([columns(blocks, h * 128), columns(blocks, 1024 + h // 2 * 128)], axis=1)


def stats_kernel(where, q0, q1, q2, q3, kc0, kc1, vs0, vs1, marks0, marks1, es, dps, stats, bias):
    xi, zi = where[0], where[1]
    blocks = (q0, q1, q2, q3)
    q_marks = jnp.concatenate([q[1280:1296, :] for q in blocks], axis=1)[0:1].astype(F32)
    lane = lax.broadcasted_iota(jnp.int32, (128, QROWS), 1)
    q_pos = zi * QROWS + ((xi + (lane >> 7)) & 3) * 128 + (lane & 127)
    for j in range(REACH):
        at = slice(j * 128, j * 128 + 128)
        first = ((zi - ORDER[j]) & (Z - 1)) * QROWS + xi * 128
        k_pos = first + lax.broadcasted_iota(jnp.int32, (128, QROWS), 0)
        allowed = (k_pos <= q_pos) & ((marks0, marks1)[j // 2][j % 2 * 128:j % 2 * 128 + 128, 64:65] == q_marks)
        bias[at, :] = jnp.where(allowed, 0.0, NEG)
    for h in range(HEADS):
        for b in range(0, QROWS, 256):
            sl = slice(b, b + 256)
            pair = blocks[b // 128:b // 128 + 2]
            qc, gs = queries_of(pair, h), columns(pair, 512 + h * 128)
            parts = []
            for n, (kc, vs) in enumerate(((kc0, vs0), (kc1, vs1))):
                at = slice(n * HALF, (n + 1) * HALF)
                s = lax.dot_general(kc[h], qc, NT, preferred_element_type=F32) * SCALE + bias[at, sl]
                dp = lax.dot_general(vs[h], gs, NT, preferred_element_type=F32)
                dps[h, at, sl] = dp
                parts.append((at, s, dp))
            m = jnp.maximum(*[jnp.max(s, axis=0, keepdims=True) for _, s, _ in parts])
            total = cross = 0.0
            for at, s, dp in parts:
                e = jnp.exp(s - m)
                es[h, at, sl] = e
                total = total + jnp.sum(e, axis=0, keepdims=True)
                cross = cross + jnp.sum(e * dp, axis=0, keepdims=True)
            stats[h:h + 1, sl] = m
            stats[4 + h:5 + h, sl] = total
            stats[8 + h:9 + h, sl] = cross
    stats[12:16, :] = jnp.zeros((4, QROWS), F32)


def run_stats(where, *mats):
    sds = jax.ShapeDtypeStruct
    return call(
        stats_kernel, (sds((4, KROWS, QROWS), F32), sds((4, KROWS, QROWS), F32), sds((16, QROWS), F32)),
        1, 10, scratch=[pltpu.VMEM((KROWS, QROWS), F32)], flops=1_000_000_000, nbytes=8 << 20,
    )(where, *mats)


def weight_kernel(where, t0, t1, t2, t3, q0, q1, q2, q3, es, dps, latents0, latents1, wk, wv, w_keep, w_far, w_send, ds, dkv, tail, d3,
                  p_scr, w_scr):
    xi, core = where[0], where[2]
    blocks = (q0, q1, q2, q3)
    ts = [t[...] if s == 0 else jnp.concatenate([t[:, 512 - s * 128:], t[:, :512 - s * 128]], axis=1)
          for s, t in enumerate((t0, t1, t2, t3))]
    tops = [t[0:4] for t in ts]
    top = functools.reduce(jnp.maximum, tops)
    total = jnp.zeros((4, QROWS), F32)
    cross = jnp.zeros((4, QROWS), F32)
    for t, m in zip(ts, tops):
        f = jnp.exp(m - top)
        total = total + f * t[4:8]
        cross = cross + f * t[8:12]
    inv = 1.0 / total
    delta = cross * inv
    scaled = jnp.exp(tops[0] - top) * inv
    rope_grad = [jnp.zeros((KROWS, 128), F32), jnp.zeros((KROWS, 128), F32)]
    for h in range(HEADS):
        p = es[h] * scaled[h:h + 1]
        p_scr[h % 2] = p.astype(BF)
        ds[h] = (p * (dps[h] - delta[h:h + 1]) * SCALE).astype(BF)
        cols = slice(h * 128, (h + 1) * 128)
        dkv[1, :, cols] = jnp.dot(p_scr[h % 2], columns(blocks, 512 + h * 128), preferred_element_type=F32).astype(BF)
        dk = jnp.dot(ds[h], queries_of(blocks, h), preferred_element_type=F32)
        dkv[0, :, cols] = dk[:, :128].astype(BF)
        rope_grad[h % 2] = rope_grad[h % 2] + dk[:, 128:]
    for out, which in ((w_scr, 1 - core), (w_keep, core)):
        w = (lax.dot_general(dkv[which, :HALF], latents0[...], TN, preferred_element_type=F32)
             + lax.dot_general(dkv[which, HALF:], latents1[...], TN, preferred_element_type=F32)).astype(BF)
        for r in range(32):
            out[(r - xi) & 3, r // 4 * 16:r // 4 * 16 + 16, :] = w[r * 16:r * 16 + 16, :]
    w_far[...] = w_scr[2]
    for n, s in enumerate((0, 1, 3)):
        w_send[n] = w_scr[s]
    lane = lax.broadcasted_iota(jnp.int32, (KROWS, 128), 1)
    tail[...] = jnp.where(lane < 64, rope_grad[0] + pltpu.roll(rope_grad[1], 64, 1), 0.0).astype(BF)
    far = slice(3 * ROWS, KROWS)
    d3[:, :512] = (lax.dot_general(dkv[0, far], wk[...], NT, preferred_element_type=F32)
                   + lax.dot_general(dkv[1, far], wv[...], NT, preferred_element_type=F32)).astype(BF)
    d3[:, 512:640] = tail[far, :]


def run_weight(where, ts, *mats):
    sds = jax.ShapeDtypeStruct
    return call(
        weight_kernel,
        (sds((4, 128, 512), BF), sds((128, 512), BF), sds((3, 128, 512), BF), sds((4, KROWS, QROWS), BF), sds((2, KROWS, 512), BF),
         sds((KROWS, 128), BF), sds((128, 640), BF)),
        1, 14, scratch=[pltpu.VMEM((2, KROWS, QROWS), BF), pltpu.VMEM((4, 128, 512), BF)], flops=1_500_000_000, nbytes=10 << 20,
    )(where, *ts, *mats)


def grads_kernel(where, ds, dkv, tail, kc0, kc1, wk, wv, d0, d1, d2, o0, o1, o2, o3, dq):
    near = slice(0, 3 * ROWS)
    lat = (lax.dot_general(dkv[0, near], wk[...], NT, preferred_element_type=F32)
           + lax.dot_general(dkv[1, near], wv[...], NT, preferred_element_type=F32)).astype(BF)
    for j, d in enumerate((d1, d2, d0)):
        d[:, :512] = lat[j * 128:(j + 1) * 128, :]
        d[:, 512:640] = tail[j * 128:(j + 1) * 128, :]
    for p in range(2):
        pair = 0.0
        for h in (2 * p, 2 * p + 1):
            dqh = (lax.dot_general(ds[h, :HALF], kc0[h], TN, preferred_element_type=F32)
                   + lax.dot_general(ds[h, HALF:], kc1[h], TN, preferred_element_type=F32))
            dq[:, h * 128:(h + 1) * 128] = dqh[:, :128].astype(BF)
            pair = pair + dqh[:, 128:]
        dq[:, 512 + p * 128:640 + p * 128] = pair.astype(BF)
    for s, o in enumerate((o0, o1, o2, o3)):
        o[...] = dq[s * 128:(s + 1) * 128, :]


def run_grads(where, ds, dkv, tail, kc0, kc1, wk, wv):
    sds = jax.ShapeDtypeStruct
    return call(
        grads_kernel,
        tuple([sds((128, 640), BF)] * 3 + [sds((128, 768), BF)] * 4),
        1, 7, scratch=[pltpu.VMEM((QROWS, 768), BF)], flops=1_500_000_000, nbytes=10 << 20,
    )(where, ds, dkv, tail, kc0, kc1, wk, wv)


def far_sum_kernel(keep, far, out):
    out[...] = (keep[2].astype(F32) + far[...].astype(F32)).astype(BF)


def near_sum_kernel(keep, near, out1, out3):
    out1[...] = (keep[1].astype(F32) + near[1].astype(F32)).astype(BF)
    out3[...] = (keep[3].astype(F32) + near[2].astype(F32)).astype(BF)


def sum_x_kernel(keep, near, p1, p2, p3, out):
    out[...] = (keep[0].astype(F32) + near[0].astype(F32) + wide(p1, p2, p3)).astype(BF)


def wide(*refs):
    return functools.reduce(jnp.add, [r[...].astype(F32) for r in refs])


def sum_kernel(*refs):
    refs[-1][...] = wide(*refs[:-1]).astype(refs[-1].dtype)


def add_up(*parts, dtype=BF):
    return call(sum_kernel, jax.ShapeDtypeStruct(parts[0].shape, dtype), 0, len(parts), nbytes=1 << 20)(*parts)


def sum_z_kernel(parts, w):
    w[...] = jnp.sum(parts[...].reshape(Z, 16, 512).astype(F32), axis=0).astype(BF)


def query_kernel(q0, q1, q2, q3, nope, rope):
    q = wide(q0, q1, q2, q3).astype(BF)
    nope[...] = q[:, :512]
    rope[...] = q[:, 512:]


def latent_kernel(part, d1, latent):
    latent[...] = wide(part, d1).astype(BF)[:, :576].T


def body(kv_latent, q_nope, q_rope, w_key_up, w_value_up, out_grad, segment_ids):
    ctx = lax.axis_index("ctx")
    dp = lax.axis_index("dp")
    core = dp % 2
    where = jnp.stack([ctx % X, ctx // X, core]).astype(jnp.int32)
    q, *c = pack(q_nope[0], q_rope[0], out_grad[0], kv_latent[0].T, segment_ids)
    c1 = [z_shift(v, 1) for v in c]
    c2 = [z_shift(v, 1) for v in c1]
    kc0, vs0, latents0, marks0, wk, wv = run_keys(c1 + c2, w_key_up, w_value_up, True)
    c3 = [z_shift(v, 1) for v in c2]
    later, _ = lax.optimization_barrier((q, c1))
    qs = (q, x_shift(q, -1), x_shift(q, 2), x_shift(later, 1))
    kc1, vs1, latents1, marks1 = run_keys(c + c3, wk, wv, False)
    es, dps, stats = run_stats(where, *qs, kc0, kc1, vs0, vs1, marks0, marks1)
    ts = (stats, x_shift(stats, -1), x_shift(stats, 2), x_shift(stats, 1))
    w_keep, w_far, w_send, ds, dkv, tail, d3 = run_weight(where, ts, *qs, es, dps, latents0, latents1, wk, wv)
    w_far, near = core_swap(w_far), core_swap(w_send)
    d0, d1, d2, o0, o1, o2, o3 = run_grads(where, ds, dkv, tail, kc0, kc1, wk, wv)
    sds = jax.ShapeDtypeStruct
    piece = sds((128, 512), BF)
    p2 = call(far_sum_kernel, piece, 0, 2, nbytes=1 << 18)(w_keep, w_far)
    p1, p3 = call(near_sum_kernel, (piece, piece), 0, 2, nbytes=1 << 19)(w_keep, near)
    w = call(sum_x_kernel, piece, 0, 5, nbytes=1 << 20)(w_keep, near, x_shift(p1, 1), x_shift(p2, 2), x_shift(p3, -1))
    w = lax.all_to_all(w, "ctx", 0, 0, tiled=True, axis_index_groups=[[z * X + x for z in range(Z)] for x in range(X)])
    d = add_up(z_shift(d3, -1), d2)
    d = call(sum_kernel, sds((128, 640), F32), 0, 2, flops=1_000_000_000, nbytes=1 << 20)(z_shift(d, -2), d0)
    w, d = lax.optimization_barrier((w, d))
    w = call(sum_z_kernel, sds((16, 512), BF), 0, 1, nbytes=1 << 18)(w)
    w = add_up(w, y_pair(w, False))
    other = y_pair(w, True)
    grad_nope, grad_rope = call(query_kernel, (sds((128, 512), BF), sds((128, 256), BF)), 0, 4, flops=1_000_000_000, nbytes=1 << 20)(
        o0, x_shift(o1, 1), x_shift(o2, 2), x_shift(o3, -1))
    grad_latent = call(latent_kernel, sds((576, 128), BF), 0, 2, nbytes=1 << 20)(d, z_shift(d1, -1))
    w, grad_latent = lax.optimization_barrier((w, grad_latent))
    w = add_up(w, other, dtype=F32)
    other = core_swap(w)
    grad_key = jnp.where(core == 0, w, other)
    grad_value = jnp.where(core == 0, other, w)
    return grad_nope[None], grad_rope[None], grad_latent.T[None], grad_key, grad_value


def solution(mesh):
    return jax.shard_map(
        body,
        mesh=mesh,
        in_specs=(
            P("dp", "ctx", None),
            P("dp", "ctx", None),
            P("dp", "ctx", None),
            P(),
            P(),
            P("dp", "ctx", None),
            P("dp", "ctx"),
        ),
        out_specs=(
            P("dp", "ctx", None),
            P("dp", "ctx", None),
            P("dp", "ctx", None),
            P("ctx", None),
            P("ctx", None),
        ),
        check_vma=False,
    )
```
